32 devices in a mesh: region: 8 (over y, x, core), ctx: 4 (over z).
Axes of the slice: x: 2, y: 2, z: 4, core: 2. Of those that a mesh axis runs over, the one named last changes fastest.
Arguments:
- tokens: bfloat16 [8, 2048, 1152], P('region', 'ctx'), may hold values from -6 to 6
- element_ids: int32 [8, 2048], P('region', 'ctx'), may hold values from 0 to 4095, as said below
- element_slot: int32 [4096], replicated, may hold values from 0 to 4095, as said below
- live_count: int32 [8, 4], P('region', 'ctx'), may hold values from 128 to 512
- cond_table: bfloat16 [4096, 1152], P(('region', 'ctx')), may hold values from -6 to 6
- w_ada: bfloat16 [1152, 3456], replicated, may hold values from -0.1875 to 0.1875
- b_ada: float32 [3456], replicated, may hold values from -3 to 3
- w_qkv: bfloat16 [1152, 3456], replicated, may hold values from -8 to 8
- w_out: bfloat16 [1152, 1152], replicated, may hold values from -0.1875 to 0.1875
Outputs:
- block_out: bfloat16 [8, 2048, 1152], P('region', 'ctx')
The draws below stay inside these ranges and needn't reach their ends.
Inputs may be any that keep to these rules, and one draw needn't show every extreme that they name: element_ids: within each device's block of 512 patches (region r, positions c * 512 to (c + 1) * 512 - 1, device r * 4 + c of region+ctx), at most 24 patches name elements whose table row lies on one device (rows o * 128 to (o + 1) * 128 - 1); in every block some device is named by exactly 24 solid patches. element_slot is a permutation: element e is row element_slot[e] of cond_table.
All inputs are finite; a program needn't handle non-finite values.
Results may differ from the reference program's by a relative error of at most 0.027.
Values may be sent and summed in bfloat16 or wider, within the bound.
No kernel may reach another device: no remote copies, remote signals or barrier semaphores. Data moves between devices by JAX's collectives and lax.ppermute only.
A program may use at most 192 MiB of HBM per device.

```python
import math
import jax
import jax.numpy as jnp
from jax import lax

D = 1152
HEADS = 16
TOK_DEV = 512
ELEM_DEV = 128
REGIONS = 8
CTX_SHARDS = 4
SEQ = 2048
OWNERS = 32
ELEMENTS = 4096
CAP = 24


def element_order(key):
    return jax.random.permutation(jax.random.fold_in(key, 17), ELEMENTS).astype(jnp.int32)


def draw_element_slot(key, part):
    return element_order(key)


def draw_element_ids(key, part):
    slot_of = element_order(key)
    element_at = jnp.argsort(slot_of, stable=True).astype(jnp.int32)
    ticket_count = CAP * OWNERS
    device_keys = jax.random.split(jax.random.fold_in(key, 23), OWNERS)

    def one_device(device_key):
        first_key, second_key = jax.random.split(device_key)
        tickets = jax.random.permutation(first_key, ticket_count).astype(jnp.int32)
        owner_of = tickets // CAP
        forced = owner_of[0]
        ranking = jnp.arange(ticket_count, dtype=jnp.int32) - ticket_count * (owner_of == forced).astype(jnp.int32)
        ordering = jnp.argsort(ranking, stable=True)
        chosen = owner_of[ordering[:TOK_DEV]]
        table_rows = jax.random.randint(second_key, (TOK_DEV,), 0, ELEM_DEV, dtype=jnp.int32)
        return element_at[chosen * ELEM_DEV + table_rows]
    return jax.vmap(one_device)(device_keys).reshape(REGIONS, SEQ)


def draw_w_qkv(key, part):
    base = jax.random.normal(key, (D, 3 * D), jnp.float32) * D ** (-0.5)
    return base.astype(jnp.bfloat16)


def place_ends(entries, own_key, smallest, top_value):
    longest = entries.shape.index(max(entries.shape))
    spots = []
    for shift in (0, 1):
        where = [jax.random.randint(jax.random.fold_in(own_key, axis), (), 0, length) for axis, length in enumerate(entries.shape)]
        where[longest] = (where[longest] + shift) % entries.shape[longest]
        spots.append(tuple(where))
    return entries.at[spots[0]].set(smallest).at[spots[1]].set(top_value)


def block_levels(rng, dims, cuts, least, top_value):
    def one(dim, parts):
        steps = jax.random.uniform(jax.random.fold_in(jax.random.fold_in(rng, 6), dim), (parts,), jnp.float32, least / len(cuts), top_value / len(cuts))
        return jnp.repeat(jnp.exp(steps), dims[dim] // parts).reshape((-1,) + (1,) * (len(dims) - dim - 1))

    gain = one(*cuts[0])
    for cut in cuts[1:]:
        gain = gain * one(*cut)
    return gain


def centred(key, shape, scale, reach, shards=(), held_as=jnp.bfloat16):
    entries = jax.random.normal(key, shape, jnp.float32) * scale
    if len(shards) > 0:
        entries = block_levels(key, shape, shards, -0.22, 0.18) * entries
    return jnp.clip(entries, min=-reach, max=reach).astype(held_as)


def setup_inputs(seed: int = 0) -> dict:
    seeds = jax.random.split(jax.random.key(seed), 10)
    tokens = centred(seeds[0], (REGIONS, SEQ, D), 1.0, 6.0, ((0, 8), (1, 4)))
    element_ids = draw_element_ids(jax.random.fold_in(seeds[9], 71), 0)
    element_slot = draw_element_slot(jax.random.fold_in(seeds[9], 71), 0)
    live_count = place_ends(jax.random.randint(seeds[3], (REGIONS, CTX_SHARDS), TOK_DEV // 4, TOK_DEV + 1), jax.random.fold_in(seeds[3], 1), TOK_DEV // 4, TOK_DEV).astype(jnp.int32)
    cond_table = centred(seeds[4], (ELEMENTS, D), 1.0, 6.0, ((0, 32),))
    w_ada = centred(seeds[5], (D, 3 * D), D ** -0.5, 0.1875)
    b_ada = centred(seeds[6], (3 * D,), 0.5, 3.0, (), jnp.float32)
    w_qkv = draw_w_qkv(jax.random.fold_in(seeds[9], 71), 0)
    w_out = centred(seeds[8], (D, D), D ** -0.5, 0.1875)
    return {"tokens": tokens, "element_ids": element_ids, "element_slot": element_slot, "live_count": live_count, "cond_table": cond_table, "w_ada": w_ada, "b_ada": b_ada, "w_qkv": w_qkv, "w_out": w_out}


def layer_modulate(region_tokens, mods, width):
    values = region_tokens.astype(jnp.float32)
    center = lax.optimization_barrier(jnp.mean(values, axis=1, keepdims=True))
    spread = lax.optimization_barrier(jnp.mean((values - center) ** 2, axis=1, keepdims=True))
    normed = (values - center) * lax.rsqrt(spread + 1e-06)
    shift = mods[:, :width]
    scale = mods[:, width:2 * width]
    return (normed * (1.0 + scale) + shift).astype(jnp.bfloat16)

def reference(tokens, element_ids, element_slot, live_count, cond_table, w_ada, b_ada, w_qkv, w_out):
    width = D
    head_dim = D // HEADS
    inverse_root = 1.0 / math.sqrt(head_dim)
    activated = jax.nn.silu(cond_table.astype(jnp.float32)).astype(jnp.bfloat16)
    table_mods = (jnp.dot(activated, w_ada, preferred_element_type=jnp.float32) + b_ada).astype(jnp.bfloat16)
    bias_row = b_ada.astype(jnp.bfloat16)
    query_block = math.gcd(SEQ, 512)

    def region_block(inputs):
        region_tokens, region_ids, region_live = inputs
        slots = element_slot[region_ids]
        position = jnp.arange(SEQ, dtype=jnp.int32)
        solid = position % TOK_DEV < jnp.repeat(region_live, TOK_DEV)
        mods = jnp.where(solid[:, None], table_mods[slots], bias_row[None, :]).astype(jnp.float32)
        modulated = layer_modulate(region_tokens, mods, width)
        qkv = jnp.dot(modulated, w_qkv, preferred_element_type=jnp.float32).astype(jnp.bfloat16)
        queries = qkv[:, :width].reshape(SEQ, HEADS, head_dim)
        keys_all = qkv[:, width:2 * width].reshape(SEQ, HEADS, head_dim).astype(jnp.float32)
        values_all = qkv[:, 2 * width:].reshape(SEQ, HEADS, head_dim).astype(jnp.float32)

        def attend_rows(query_rows):
            scores = jnp.einsum('qhe,khe->hqk', query_rows.astype(jnp.float32), keys_all) * inverse_root
            peak = lax.optimization_barrier(jnp.max(scores, axis=2, keepdims=True))
            expo = jnp.exp(scores - peak)
            denominator = lax.optimization_barrier(jnp.sum(expo, axis=2))
            weights = expo.astype(jnp.bfloat16).astype(jnp.float32)
            summed = jnp.einsum('hqk,khe->hqe', weights, values_all)
            result = summed / denominator[:, :, None]
            return jnp.transpose(result, (1, 0, 2)).reshape(query_rows.shape[0], width).astype(jnp.bfloat16)
        attended = lax.map(attend_rows, queries.reshape(SEQ // query_block, query_block, HEADS, head_dim))
        attended = attended.reshape(SEQ, width)
        projected = jnp.dot(attended, w_out, preferred_element_type=jnp.float32)
        gate = mods[:, 2 * width:]
        return (region_tokens.astype(jnp.float32) + gate * projected).astype(jnp.bfloat16)
    return lax.map(region_block, (tokens, element_ids, live_count))
```

```python
import functools
import math

import jax
import jax.numpy as jnp
from jax import lax
from jax.experimental import pallas as pl
from jax.experimental.pallas import tpu as pltpu
from jax.sharding import PartitionSpec as P

HEADS = 16
F32 = jnp.float32
BF16 = jnp.bfloat16
VMEM_LIMIT = 56 * 2**20


def contract(a, b, dims):
    return lax.dot_general(a, b, (dims, ((), ())), preferred_element_type=F32)


def pick_kernel(bases, count, idx_ref, acc_ref, *refs):
    pieces, (out_ref, rows_ref) = refs[:-2], refs[-2:]
    rows = pieces[0].shape[0]

    @pl.when(pl.program_id(0) == 0)
    def _():
        for n, piece in enumerate(pieces):
            rows_ref[n * rows : (n + 1) * rows, :] = piece[...]

    idx = idx_ref[...]
    lane = lax.broadcasted_iota(jnp.int32, (1, rows), 1)
    hot = jnp.concatenate(
        [jnp.where(idx == lane + base, 1.0, 0.0).astype(BF16) for base in bases], axis=1
    )
    picked = contract(hot, rows_ref[...], ((1,), (0,)))
    out_ref[...] = (picked + acc_ref[...].astype(F32)).astype(BF16)


def pick_rows(idx, acc, pieces, bases, block):
    count, width = acc.shape
    rows = pieces[0].shape[0]
    return pl.pallas_call(
        functools.partial(pick_kernel, bases, count),
        grid=(count // block,),
        in_specs=[
            pl.BlockSpec((block, 1), lambda i: (i, 0)),
            pl.BlockSpec((block, width), lambda i: (i, 0)),
        ]
        + [
            pl.BlockSpec((rows, width), lambda i: (0, 0), pipeline_mode=pl.Buffered(1))
            for _ in pieces
        ],
        out_specs=pl.BlockSpec((block, width), lambda i: (i, 0)),
        out_shape=jax.ShapeDtypeStruct((count, width), BF16),
        scratch_shapes=[pltpu.VMEM((len(pieces) * rows, width), BF16)],
        input_output_aliases={1: 0},
        compiler_params=pltpu.CompilerParams(vmem_limit_bytes=VMEM_LIMIT),
        cost_estimate=pl.CostEstimate(
            flops=2 * count * len(pieces) * rows * width,
            bytes_accessed=2 * width * (2 * count + len(pieces) * rows),
            transcendentals=0,
        ),
        name="pick",
    )(idx, acc, *pieces)


def project_kernel(
    query_scale, place_ref, tok_ref, act_ref, wada_ref, bada_ref, wt_ref, kv_ref, q_ref, gate_ref
):
    width = tok_ref.shape[1]
    values = tok_ref[...].astype(F32)
    center = jnp.mean(values, axis=1, keepdims=True)
    moved = values - center
    spread = jnp.mean(moved * moved, axis=1, keepdims=True)
    normed = moved * lax.rsqrt(spread + 1e-06)
    act = jax.nn.silu(act_ref[...].astype(F32)).astype(BF16)

    def mods(lo):
        part = contract(act, wada_ref[:, lo : lo + width], ((1,), (0,)))
        return (part + bada_ref[:, lo : lo + width]).astype(BF16)

    shift = mods(0).astype(F32)
    scale = mods(width).astype(F32)
    modulated = (normed * (1.0 + scale) + shift).astype(BF16)
    kv_ref[...] = contract(wt_ref[width:, :], modulated, ((1,), (1,))).astype(BF16)
    i = pl.program_id(0)

    @pl.when((i >= place_ref[0]) & (i < place_ref[0] + 2))
    def _():
        gate_ref[...] = mods(2 * width)
        q_ref[...] = (contract(wt_ref[:width, :], modulated, ((1,), (1,))) * query_scale).astype(
            BF16
        )


def project(place, tok, act, w_ada, b_ada, wt, block):
    count, width = tok.shape
    query_scale = math.log2(math.e) / math.sqrt(width // HEADS)

    def mine(i, place):
        return jnp.clip(i - place[0], 0, 1) ^ place[1]

    def fixed(shape):
        return pl.BlockSpec(shape, lambda i, place: (0, 0), pipeline_mode=pl.Buffered(1))

    return pl.pallas_call(
        functools.partial(project_kernel, query_scale),
        grid_spec=pltpu.PrefetchScalarGridSpec(
            num_scalar_prefetch=1,
            grid=(count // block,),
            in_specs=[
                pl.BlockSpec((block, width), lambda i, place: (i, 0)),
                pl.BlockSpec((block, width), lambda i, place: (i, 0)),
                fixed(w_ada.shape),
                fixed(b_ada.shape),
                fixed(wt.shape),
            ],
            out_specs=[
                pl.BlockSpec((2 * width, block), lambda i, place: (0, i)),
                pl.BlockSpec((width, block), lambda i, place: (0, mine(i, place))),
                pl.BlockSpec((block, width), lambda i, place: (mine(i, place), 0)),
            ],
        ),
        out_shape=[
            jax.ShapeDtypeStruct((2 * width, count), BF16),
            jax.ShapeDtypeStruct((width, 2 * block), BF16),
            jax.ShapeDtypeStruct((2 * block, width), BF16),
        ],
        compiler_params=pltpu.CompilerParams(vmem_limit_bytes=VMEM_LIMIT),
        name="project",
    )(place, tok, act, w_ada, b_ada, wt)


def attend_kernel(head_dim, chunk, q_ref, ka_ref, kb_ref, va_ref, vb_ref, o_ref, s_ref):
    pair = q_ref.shape[0]
    row = lax.broadcasted_iota(jnp.int32, (pair, 1), 0)
    q = q_ref[...]
    parts = [(ka_ref, va_ref, i) for i in range(0, ka_ref.shape[1], chunk)]
    parts += [(kb_ref, vb_ref, i) for i in range(0, kb_ref.shape[1], chunk)]
    results = []
    for j in range(2):
        own = (row >= head_dim) if j else (row < head_dim)
        head_q = jnp.where(own, q, jnp.zeros_like(q))
        top = None
        for n, (k_ref, _, i) in enumerate(parts):
            scores = contract(k_ref[:, i : i + chunk], head_q, ((0,), (0,)))
            s_ref[j, n * chunk : (n + 1) * chunk, :] = scores
            peak = jnp.max(scores, axis=0, keepdims=True)
            top = peak if top is None else jnp.maximum(top, peak)
        weighted = denominator = None
        for n, (_, v_ref, i) in enumerate(parts):
            expo = jnp.exp2(s_ref[j, n * chunk : (n + 1) * chunk, :] - top)
            total = jnp.sum(expo, axis=0, keepdims=True)
            part = contract(v_ref[:, i : i + chunk], expo.astype(BF16), ((1,), (0,)))
            weighted = part if weighted is None else weighted + part
            denominator = total if denominator is None else denominator + total
        results.append(weighted / denominator)
    o_ref[...] = jnp.where(row < head_dim, results[0], results[1]).astype(BF16)


def attend(qt, kv_here, kv_there):
    width, queries = qt.shape
    keys = kv_here.shape[1]
    head_dim = width // HEADS
    pair, pairs = 2 * head_dim, HEADS // 2
    chunk = math.gcd(keys, 1024)
    first = pl.BlockSpec((pair, keys), lambda p: (p, 0))
    second = pl.BlockSpec((pair, keys), lambda p: (p + pairs, 0))
    return pl.pallas_call(
        functools.partial(attend_kernel, head_dim, chunk),
        grid=(pairs,),
        in_specs=[pl.BlockSpec((pair, queries), lambda p: (p, 0)), first, first, second, second],
        out_specs=pl.BlockSpec((pair, queries), lambda p: (p, 0)),
        out_shape=jax.ShapeDtypeStruct((width, queries), BF16),
        scratch_shapes=[pltpu.VMEM((2, 2 * keys, queries), F32)],
        compiler_params=pltpu.CompilerParams(vmem_limit_bytes=VMEM_LIMIT),
        name="attend",
    )(qt, kv_here, kv_there, kv_here, kv_there)


def finish_kernel(place_ref, att_ref, tok_ref, gate_ref, w_ref, o_ref):
    projected = contract(att_ref[...], w_ref[...], ((0,), (0,)))
    o_ref[...] = (tok_ref[...].astype(F32) + gate_ref[...].astype(F32) * projected).astype(BF16)


def finish(place, attended, tok, gate, w_out, block):
    width, queries = attended.shape
    return pl.pallas_call(
        finish_kernel,
        grid_spec=pltpu.PrefetchScalarGridSpec(
            num_scalar_prefetch=1,
            grid=(queries // block,),
            in_specs=[
                pl.BlockSpec((width, block), lambda i, place: (0, i)),
                pl.BlockSpec((block, width), lambda i, place: (place[0] + (i ^ place[1]), 0)),
                pl.BlockSpec((block, width), lambda i, place: (i, 0)),
                pl.BlockSpec((width, width), lambda i, place: (0, 0)),
            ],
            out_specs=pl.BlockSpec((block, width), lambda i, place: (i, 0)),
        ),
        out_shape=jax.ShapeDtypeStruct((queries, width), BF16),
        compiler_params=pltpu.CompilerParams(vmem_limit_bytes=VMEM_LIMIT),
        name="finish",
    )(place, attended, tok, gate, w_out)


def swap(x, axis, bits):
    return lax.ppermute(x, axis, [(i, i ^ bits) for i in range(lax.axis_size(axis))])


def spread_table(own):
    size = lax.axis_size("region")
    bits = [1 << n for n in range(1, size.bit_length() - 1)]
    blocks = {0: own}
    for bit in bits[2:]:
        blocks.update({o ^ bit: swap(b, "region", bit) for o, b in list(blocks.items())})
    if len(bits) >= 2:
        first, second = bits[:2]
        half = own.shape[0] // 2
        for o, b in list(blocks.items()):
            one, two = swap(b, "region", first), swap(b, "region", second)
            low = swap(two[:half], "region", first)
            high = swap(one[half:], "region", second)
            blocks[o ^ first], blocks[o ^ second] = one, two
            blocks[o ^ first ^ second] = jnp.concatenate([low, high], axis=0)
    elif bits:
        blocks.update({o ^ bits[0]: swap(b, "region", bits[0]) for o, b in list(blocks.items())})
    blocks.update({o ^ 1: swap(b, "region", 1) for o, b in list(blocks.items())})
    return [blocks[o] for o in range(size)]


def per_device(
    tokens, element_ids, element_slot, live_count, cond_table, w_ada, b_ada, w_qkv, w_out
):
    device_tokens = tokens[0]
    tok_rows, width = device_tokens.shape
    elem_rows = cond_table.shape[0]
    n = lax.axis_size("ctx")
    h = n // 2
    block = tok_rows // 2
    r, c = lax.axis_index("region"), lax.axis_index("ctx")
    core, upper = r % 2, (c >= h).astype(jnp.int32)
    m = jnp.where(upper == 1, n - 1 - c, c)

    slot = element_slot[element_ids[0]]
    position = jnp.arange(tok_rows, dtype=jnp.int32)
    slot = jnp.where(position < live_count[0, 0], slot, -1)
    slots = jnp.stack([slot] + [swap(slot, "ctx", d) for d in range(1, n)])
    slots = jnp.where(core == upper, slots, swap(slots, "region", 1))
    slots = lax.dynamic_slice_in_dim(slots, core * block, block, axis=1)
    shard = jnp.arange(n, dtype=jnp.int32)
    shard = jnp.where(shard < h, shard ^ m, shard)
    shard_ctx = jnp.where(upper == 1, n - 1 - shard, shard)
    slots = jnp.take(slots, shard_ctx ^ c, axis=0).reshape(n * block, 1)
    owner = slots // elem_rows
    relative = ((((owner // n) ^ r) * n) + ((owner % n) ^ c)) * elem_rows + slots % elem_rows
    relative = jnp.where(slots < 0, -1, relative)

    mine = lax.dynamic_slice_in_dim(device_tokens, core * block, block)
    other = lax.dynamic_slice_in_dim(device_tokens, (1 - core) * block, block)
    got = swap(other, "region", 1)
    even, odd = jnp.where(core == 0, mine, got), jnp.where(core == 0, got, mine)
    work, pass_on = jnp.where(upper == 0, even, odd), jnp.where(upper == 0, odd, even)
    arrived = [work] + [swap(work, "ctx", d) for d in range(1, h)]
    for j in range(h):
        piece = lax.ppermute(pass_on, "ctx", [(h + j, h - 1), (h - 1 - j, h)])
        held = piece
        for k in range(h - 1, 0, -1):
            piece = lax.ppermute(piece, "ctx", [(k, k - 1), (n - 1 - k, n - k)])
            held = jnp.where(m == k - 1, piece, held)
        arrived.append(held)
    tok = jnp.concatenate(arrived, axis=0)

    picked = jnp.zeros((n * block, width), BF16)
    near = spread_table(cond_table)
    far = spread_table(
        jnp.concatenate([swap(cond_table, "ctx", d) for d in range(1, n)], axis=0)
    )
    size = lax.axis_size("region")
    near_bases = [o * n * elem_rows for o in range(size)]
    picked = pick_rows(relative, picked, near, near_bases, block)
    step = len(far) if n == 4 else 4
    for lo in range(0, len(far), step):
        far_bases = [(o * n + 1) * elem_rows for o in range(lo, lo + step)]
        picked = pick_rows(relative, picked, far[lo : lo + step], far_bases, block)

    base = jnp.where(2 * m < h, (2 * m) ^ m, 2 * m) & ~1
    flip = jnp.where(2 * m < h, m & 1, 0)
    place = jnp.stack([base, flip]).astype(jnp.int32)
    kv, qt, gate = project(place, tok, picked, w_ada, b_ada.reshape(1, -1), w_qkv.T, block)
    attended = attend(qt, kv, swap(kv, "region", 1))
    result = finish(place, attended, tok, gate, w_out, block)

    home = []
    for i in range(2):
        pairs = [(k, 2 * k + i) for k in range(h)]
        pairs += [(n - 1 - a, n - 1 - b) for a, b in pairs]
        home.append(lax.ppermute(result[i * block : (i + 1) * block], "ctx", pairs))
    parity = c % 2
    even = jnp.where(parity == 0, home[0], home[1])
    odd = jnp.where(parity == 0, home[1], home[0])
    mine = jnp.where(core == 0, even, odd)
    got = swap(jnp.where(core == 0, odd, even), "region", 1)
    low, high = jnp.where(core == 0, mine, got), jnp.where(core == 0, got, mine)
    return jnp.concatenate([low, high], axis=0)[None]


def solution(mesh):
    placed = (
        P("region", "ctx", None),
        P("region", "ctx"),
        P(),
        P("region", "ctx"),
        P(("region", "ctx"), None),
        P(),
        P(),
        P(),
        P(),
    )
    return jax.shard_map(
        per_device, mesh=mesh, in_specs=placed, out_specs=P("region", "ctx", None), check_vma=False
    )
```

```python
import functools
import math

import jax
import jax.numpy as jnp
from jax import lax
from jax.experimental import pallas as pl
from jax.experimental.pallas import tpu as pltpu
from jax.sharding import PartitionSpec as P

HEADS = 16
F32 = jnp.float32
BF16 = jnp.bfloat16
VMEM_LIMIT = 56 * 2**20


def contract(a, b, dims):
    return lax.dot_general(a, b, (dims, ((), ())), preferred_element_type=F32)


def pick_kernel(bases, count, idx_ref, acc_ref, *refs):
    pieces, (out_ref, rows_ref) = refs[:-2], refs[-2:]
    rows = pieces[0].shape[0]

    @pl.when(pl.program_id(0) == 0)
    def _():
        for n, piece in enumerate(pieces):
            rows_ref[n * rows : (n + 1) * rows, :] = piece[...]

    idx = idx_ref[...]
    lane = lax.broadcasted_iota(jnp.int32, (1, rows), 1)
    hot = jnp.concatenate(
        [jnp.where(idx == lane + base, 1.0, 0.0).astype(BF16) for base in bases], axis=1
    )
    picked = contract(hot, rows_ref[...], ((1,), (0,)))
    out_ref[...] = (picked + acc_ref[...].astype(F32)).astype(BF16)


def pick_rows(idx, acc, pieces, bases, block):
    count, width = acc.shape
    rows = pieces[0].shape[0]
    return pl.pallas_call(
        functools.partial(pick_kernel, bases, count),
        grid=(count // block,),
        in_specs=[
            pl.BlockSpec((block, 1), lambda i: (i, 0)),
            pl.BlockSpec((block, width), lambda i: (i, 0)),
        ]
        + [
            pl.BlockSpec((rows, width), lambda i: (0, 0), pipeline_mode=pl.Buffered(1))
            for _ in pieces
        ],
        out_specs=pl.BlockSpec((block, width), lambda i: (i, 0)),
        out_shape=jax.ShapeDtypeStruct((count, width), BF16),
        scratch_shapes=[pltpu.VMEM((len(pieces) * rows, width), BF16)],
        input_output_aliases={1: 0},
        compiler_params=pltpu.CompilerParams(vmem_limit_bytes=VMEM_LIMIT),
        cost_estimate=pl.CostEstimate(flops=1, bytes_accessed=1, transcendentals=0),
        name="pick",
    )(idx, acc, *pieces)


def stretch_kernel(
    steps, tok_ref, act_ref, ws_ref, wc_ref, bs_ref, bc_ref, w_ref, kv_ref, x_ref, norm_ref, silu_ref
):
    i = pl.program_id(0)
    cols = ws_ref.shape[1]

    @pl.when(i == 0)
    def _():
        values = tok_ref[...].astype(F32)
        moved = values - jnp.mean(values, axis=1, keepdims=True)
        spread = jnp.mean(moved * moved, axis=1, keepdims=True)
        norm_ref[...] = moved * lax.rsqrt(spread + 1e-06)
        silu_ref[...] = jax.nn.silu(act_ref[...].astype(F32)).astype(BF16)

    for step in range(steps):

        @pl.when(i == step)
        def _():
            act = silu_ref[...]
            shift = (contract(act, ws_ref[...], ((1,), (0,))) + bs_ref[...]).astype(BF16)
            scale = (contract(act, wc_ref[...], ((1,), (0,))) + bc_ref[...]).astype(BF16)
            span = slice(step * cols, (step + 1) * cols)
            x_ref[:, span] = (
                norm_ref[:, span] * (1.0 + scale.astype(F32)) + shift.astype(F32)
            ).astype(BF16)

    @pl.when(i >= steps)
    def _():
        kv_ref[...] = contract(w_ref[...], x_ref[...], ((0,), (1,))).astype(BF16)


def stretch(tok, picked, w_ada, b_ada, w_qkv, first, count):
    width = tok.shape[1]
    cols, rows = width // 3, width
    steps, kv_steps = width // cols, 2 * width // rows
    at = first // count

    def ada(i):
        return jnp.minimum(i, steps - 1)

    def kv(i):
        return jnp.maximum(i - steps, 0)

    return pl.pallas_call(
        functools.partial(stretch_kernel, steps),
        grid=(steps + kv_steps,),
        in_specs=[
            pl.BlockSpec((count, width), lambda i: (0, 0)),
            pl.BlockSpec((count, width), lambda i: (at, 0)),
            pl.BlockSpec((width, cols), lambda i: (0, ada(i))),
            pl.BlockSpec((width, cols), lambda i: (0, ada(i) + steps)),
            pl.BlockSpec((1, cols), lambda i: (0, ada(i))),
            pl.BlockSpec((1, cols), lambda i: (0, ada(i) + steps)),
            pl.BlockSpec((width, rows), lambda i: (0, kv(i) + width // rows)),
        ],
        out_specs=[
            pl.BlockSpec((rows, count), lambda i: (kv(i), 0)),
            pl.BlockSpec((count, width), lambda i: (0, 0)),
        ],
        out_shape=[
            jax.ShapeDtypeStruct((2 * width, count), BF16),
            jax.ShapeDtypeStruct((count, width), BF16),
        ],
        scratch_shapes=[pltpu.VMEM((count, width), F32), pltpu.VMEM((count, width), BF16)],
        compiler_params=pltpu.CompilerParams(vmem_limit_bytes=VMEM_LIMIT),
        cost_estimate=pl.CostEstimate(flops=1, bytes_accessed=1, transcendentals=0),
        name="stretch",
    )(tok, picked, w_ada, w_ada, b_ada, b_ada, w_qkv)


def query_kernel(query_scale, place_ref, x_ref, act_ref, wg_ref, bg_ref, w_ref, q_ref, gate_ref):
    act = jax.nn.silu(act_ref[...].astype(F32)).astype(BF16)
    gate_ref[...] = (contract(act, wg_ref[...], ((1,), (0,))) + bg_ref[...]).astype(BF16)
    q = contract(w_ref[...], x_ref[...], ((0,), (1,)))
    q_ref[...] = (q * query_scale).astype(BF16)


def query(place, x, picked, w_ada, b_ada, w_qkv):
    count, width = x.shape
    query_scale = math.log2(math.e) / math.sqrt(width // HEADS)
    cols = width // 3
    last = 2 * width // cols
    return pl.pallas_call(
        functools.partial(query_kernel, query_scale),
        grid_spec=pltpu.PrefetchScalarGridSpec(
            num_scalar_prefetch=1,
            grid=(width // cols,),
            in_specs=[
                pl.BlockSpec((count, width), lambda i, place: (0, 0)),
                pl.BlockSpec((count, width), lambda i, place: (place[0] // 2, 0)),
                pl.BlockSpec((width, cols), lambda i, place: (0, i + last)),
                pl.BlockSpec((1, cols), lambda i, place: (0, i + last)),
                pl.BlockSpec((width, cols), lambda i, place: (0, i)),
            ],
            out_specs=[
                pl.BlockSpec((cols, count), lambda i, place: (i, 0)),
                pl.BlockSpec((count, cols), lambda i, place: (0, i)),
            ],
        ),
        out_shape=[
            jax.ShapeDtypeStruct((width, count), BF16),
            jax.ShapeDtypeStruct((count, width), BF16),
        ],
        compiler_params=pltpu.CompilerParams(vmem_limit_bytes=VMEM_LIMIT),
        cost_estimate=pl.CostEstimate(
            flops=4 * count * width * width, bytes_accessed=4 * width * width, transcendentals=0
        ),
        name="query",
    )(place, x, picked, w_ada, b_ada, w_qkv)


def attend_kernel(head_dim, chunk, place_ref, q_ref, *refs):
    kv_refs, (o_ref, s_ref) = refs[:-2], refs[-2:]
    pair, queries = q_ref.shape
    row = lax.broadcasted_iota(jnp.int32, (pair, 1), 0)
    q = q_ref[...]
    zero = jnp.zeros_like(q)
    both = jnp.concatenate(
        [jnp.where(row < head_dim, q, zero), jnp.where(row < head_dim, zero, q)], axis=1
    )
    half = len(kv_refs) // 2
    parts = [
        (k_ref, v_ref, i)
        for k_ref, v_ref in zip(kv_refs[:half], kv_refs[half:])
        for i in range(0, k_ref.shape[1], chunk)
    ]
    top = None
    for n, (k_ref, _, i) in enumerate(parts):
        scores = contract(k_ref[:, i : i + chunk], both, ((0,), (0,)))
        s_ref[n * chunk : (n + 1) * chunk, :] = scores
        peak = jnp.max(scores, axis=0, keepdims=True)
        top = peak if top is None else jnp.maximum(top, peak)
    weighted = denominator = None
    for n, (_, v_ref, i) in enumerate(parts):
        expo = jnp.exp2(s_ref[n * chunk : (n + 1) * chunk, :] - top)
        total = jnp.sum(expo, axis=0, keepdims=True)
        part = contract(v_ref[:, i : i + chunk], expo.astype(BF16), ((1,), (0,)))
        weighted = part if weighted is None else weighted + part
        denominator = total if denominator is None else denominator + total
    result = weighted / denominator
    o_ref[...] = jnp.where(row < head_dim, result[:, :queries], result[:, queries:]).astype(BF16)


def attend(place, which, qt, kvs):
    width, queries = qt.shape[0], qt.shape[1] // 2
    keys = kvs[0].shape[1]
    head_dim = width // HEADS
    pair, pairs = 2 * head_dim, HEADS // 2
    chunk = math.gcd(keys, 512)
    k_spec = pl.BlockSpec((pair, keys), lambda p, place: (p, 0))
    v_spec = pl.BlockSpec((pair, keys), lambda p, place: (p + pairs, 0))
    total = len(kvs) * keys
    return pl.pallas_call(
        functools.partial(attend_kernel, head_dim, chunk),
        grid_spec=pltpu.PrefetchScalarGridSpec(
            num_scalar_prefetch=1,
            grid=(pairs,),
            in_specs=[pl.BlockSpec((pair, queries), lambda p, place: (p, place[which]))]
            + [k_spec] * len(kvs)
            + [v_spec] * len(kvs),
            out_specs=pl.BlockSpec((pair, queries), lambda p, place: (p, 0)),
            scratch_shapes=[pltpu.VMEM((total, 2 * queries), F32)],
        ),
        out_shape=jax.ShapeDtypeStruct((width, queries), BF16),
        compiler_params=pltpu.CompilerParams(vmem_limit_bytes=VMEM_LIMIT),
        cost_estimate=pl.CostEstimate(
            flops=16 * total * queries * width,
            bytes_accessed=4 * total * width,
            transcendentals=HEADS * total * queries,
        ),
        name="attend",
    )(place, qt, *kvs, *kvs)


def finish_kernel(place_ref, att_ref, tok_ref, gate_ref, w_ref, o_ref):
    projected = contract(att_ref[...], w_ref[...], ((0,), (0,)))
    o_ref[...] = (tok_ref[...].astype(F32) + gate_ref[...].astype(F32) * projected).astype(BF16)


def finish(place, which, attended, tok, gate, w_out):
    width, queries = attended.shape
    at = pl.BlockSpec((queries, width), lambda i, place: (place[which], 0))
    return pl.pallas_call(
        finish_kernel,
        grid_spec=pltpu.PrefetchScalarGridSpec(
            num_scalar_prefetch=1,
            grid=(1,),
            in_specs=[
                pl.BlockSpec((width, queries), lambda i, place: (0, 0)),
                at,
                at,
                pl.BlockSpec((width, width), lambda i, place: (0, 0)),
            ],
            out_specs=pl.BlockSpec((queries, width), lambda i, place: (0, 0)),
        ),
        out_shape=jax.ShapeDtypeStruct((queries, width), BF16),
        compiler_params=pltpu.CompilerParams(vmem_limit_bytes=VMEM_LIMIT),
        name="finish",
    )(place, attended, tok, gate, w_out)


def swap(x, axis, bits):
    return lax.ppermute(x, axis, [(i, i ^ bits) for i in range(lax.axis_size(axis))])


def after(x, *others):
    return lax.optimization_barrier((x, others))[0]


def to_chips(own):
    return {o: swap(own, "region", o) if o else own for o in range(0, lax.axis_size("region"), 2)}


def to_cores(blocks):
    both = blocks | {o ^ 1: swap(b, "region", 1) for o, b in blocks.items()}
    return [both[o] for o in range(len(both))]


def per_device(
    tokens, element_ids, element_slot, live_count, cond_table, w_ada, b_ada, w_qkv, w_out
):
    device_tokens = tokens[0]
    tok_rows, width = device_tokens.shape
    elem_rows = cond_table.shape[0]
    size, n = lax.axis_size("region"), lax.axis_size("ctx")
    h = n // 2
    block = tok_rows // 2
    r, c = lax.axis_index("region"), lax.axis_index("ctx")
    core, upper = r % 2, (c >= h).astype(jnp.int32)
    m = jnp.where(upper == 1, n - 1 - c, c)

    tables = [swap(cond_table, "ctx", d) for d in range(1, n)]
    near = to_chips(cond_table)
    mine = lax.dynamic_slice_in_dim(device_tokens, core * block, block)
    other = lax.dynamic_slice_in_dim(device_tokens, (1 - core) * block, block)
    got = swap(other, "region", 1)
    position = jnp.arange(tok_rows, dtype=jnp.int32)
    ids = jnp.where(position < live_count[0, 0], element_ids[0], -1)
    ids = [ids] + [swap(ids, "ctx", d) for d in range(1, n)]
    tables, near, mine, got, ids = lax.optimization_barrier((tables, near, mine, got, ids))

    even, odd = jnp.where(core == 0, mine, got), jnp.where(core == 0, got, mine)
    work, pass_on = jnp.where(upper == 0, even, odd), jnp.where(upper == 0, odd, even)
    far = to_chips(jnp.concatenate(tables, axis=0))
    arrived = [work] + [swap(work if d < h else pass_on, "ctx", d) for d in range(1, n)]

    ids = jnp.stack(ids)
    ids = jnp.where(core == upper, ids, swap(ids, "region", 1))
    ids = lax.dynamic_slice_in_dim(ids, core * block, block, axis=1)
    ids = ids.reshape(n * block, 1)
    slots = element_slot[jnp.maximum(ids, 0)]
    owner = slots // elem_rows
    relative = ((((owner // n) ^ r) * n) + ((owner % n) ^ c)) * elem_rows + slots % elem_rows
    relative = jnp.where(ids < 0, -1, relative)

    def pick(picked, pieces, d):
        bases = [(o * n + d) * elem_rows for o in range(size)]
        return pick_rows(relative, picked, pieces, bases, 2 * block)

    picked = jnp.zeros((n * block, width), BF16)
    picked = pick(picked, to_cores(near), 0)
    far, picked = lax.optimization_barrier((far, picked))
    far = to_cores(far)
    for lo in range(0, size, 8):
        bases = [(o * n + 1) * elem_rows for o in range(lo, lo + 8)]
        picked = pick_rows(relative, picked, far[lo : lo + 8], bases, 2 * block)

    base, flip = ((2 * m) ^ m) & ~1, m & 1
    place = jnp.stack([base, core ^ flip, 1 - core ^ flip]).astype(jnp.int32)
    bias = b_ada.reshape(1, -1)
    kvs, xs, toks = [], [], []
    for at in range(0, n, 2):
        tok = jnp.concatenate(arrived[at : at + 2], axis=0)
        kv, x = stretch(tok, picked, w_ada, bias, w_qkv, at * block, 2 * block)
        kvs += [kv, swap(kv, "region", 1)]
        xs.append(x)
        toks.append(tok)
    x, tok = xs[0], toks[0]
    for at in range(1, n // 2):
        here = base == 2 * at
        x, tok = jnp.where(here, xs[at], x), jnp.where(here, toks[at], tok)
    qt, gate = query(place, x, picked, w_ada, bias, w_qkv)

    home = []
    for which in (1, 2):
        attended = attend(place, which, qt, kvs)
        result = finish(place, which, attended, tok, gate, w_out)
        pairs = []
        for region in range(size):
            for k in range(h):
                to = 2 * k + (region % 2 if which == 1 else 1 - region % 2)
                pairs.append((region * n + k, (region & ~1) * n + to))
                pairs.append((region * n + n - 1 - k, (region | 1) * n + n - 1 - to))
        home.append(lax.ppermute(result, ("region", "ctx"), pairs))
    number = jnp.where(core == 1, n - 1 - c, c) % 2
    low, high = jnp.where(number == 0, home[0], home[1]), jnp.where(number == 0, home[1], home[0])
    return jnp.concatenate([low, high], axis=0)[None]


def solution(mesh):
    placed = (
        P("region", "ctx", None),
        P("region", "ctx"),
        P(),
        P("region", "ctx"),
        P(("region", "ctx"), None),
        P(),
        P(),
        P(),
        P(),
    )
    return jax.shard_map(
        per_device, mesh=mesh, in_specs=placed, out_specs=P("region", "ctx", None), check_vma=False
    )
```

```python
import functools
import math

import jax
import jax.numpy as jnp
from jax import lax
from jax.experimental import pallas as pl
from jax.experimental.pallas import tpu as pltpu
from jax.sharding import PartitionSpec as P

HEADS = 16
F32 = jnp.float32
BF16 = jnp.bfloat16
MIB = 2**20


def contract(a, b, dims):
    return lax.dot_general(a, b, (dims, ((), ())), preferred_element_type=F32)


VMEM = pl.BlockSpec(memory_space=pltpu.VMEM)
HBM = pl.BlockSpec(memory_space=pltpu.HBM)


def pick_kernel(bases, block, idx_ref, *refs):
    pieces, (out_ref, rows_ref) = refs[:-2], refs[-2:]
    acc_ref = None
    if len(pieces) > len(bases):
        acc_ref, pieces = pieces[0], pieces[1:]
    rows = pieces[0].shape[0]
    for n, piece in enumerate(pieces):
        rows_ref[n * rows : (n + 1) * rows, :] = piece[...]
    lane = lax.broadcasted_iota(jnp.int32, (1, rows), 1)
    for lo in range(0, out_ref.shape[0], block):
        span = slice(lo, lo + block)
        idx = idx_ref[span, :]
        hot = jnp.concatenate(
            [jnp.where(idx == lane + base, 1.0, 0.0).astype(BF16) for base in bases], axis=1
        )
        picked = contract(hot, rows_ref[...], ((1,), (0,)))
        if acc_ref is not None:
            picked = picked + acc_ref[span, :].astype(F32)
        out_ref[span, :] = picked.astype(BF16)


def pick_rows(idx, acc, pieces, bases, block):
    rows, width = pieces[0].shape
    return pl.pallas_call(
        functools.partial(pick_kernel, bases, block),
        in_specs=[VMEM] * (1 + len(acc) + len(pieces)),
        out_specs=VMEM,
        out_shape=jax.ShapeDtypeStruct((idx.shape[0], width), BF16),
        scratch_shapes=[pltpu.VMEM((len(pieces) * rows, width), BF16)],
        input_output_aliases={1: 0} if acc else {},
        compiler_params=pltpu.CompilerParams(vmem_limit_bytes=16 * MIB),
        cost_estimate=pl.CostEstimate(flops=1, bytes_accessed=1, transcendentals=0),
        name="pick",
    )(idx, *acc, *pieces)


def stretch_kernel(steps, act_ref, wa_ref, ba_ref, tok_ref, wq_ref, kv_ref, x_ref, *scratch):
    tok_buf, wq_buf, silu_ref, mods_ref, sems = scratch
    count, width = x_ref.shape
    cols = wa_ref.shape[1]
    i = pl.program_id(0)
    tok_copy = pltpu.make_async_copy(tok_ref, tok_buf, sems.at[0])
    wq_copies = [
        pltpu.make_async_copy(
            wq_ref.at[:, k * width : (k + 1) * width], wq_buf.at[k - 1], sems.at[k]
        )
        for k in (1, 2)
    ]
    blocks = [slice(lo, lo + 256) for lo in range(0, count, 256)]

    @pl.when(i == 0)
    def _():
        tok_copy.start()
        for copy in wq_copies:
            copy.start()
        for span in blocks:
            silu_ref[span, :] = jax.nn.silu(act_ref[span, :].astype(F32)).astype(BF16)

    for k in range(steps):

        @pl.when(i == k)
        def _():
            mods = contract(silu_ref[...], wa_ref[...], ((1,), (0,))) + ba_ref[...]
            mods_ref[:, k * cols : (k + 1) * cols] = mods.astype(BF16)

    @pl.when(i == steps - 1)
    def _():
        tok_copy.wait()
        for span in blocks:
            values = tok_buf[span, :].astype(F32)
            moved = values - jnp.mean(values, axis=1, keepdims=True)
            spread = jnp.mean(moved * moved, axis=1, keepdims=True)
            normed = moved * lax.rsqrt(spread + 1e-06)
            shift, scale = mods_ref[span, :width], mods_ref[span, width:]
            x_ref[span, :] = (normed * (1.0 + scale.astype(F32)) + shift.astype(F32)).astype(BF16)

    for k, copy in enumerate(wq_copies):

        @pl.when(i == steps + k)
        def _():
            copy.wait()
            kv_ref[...] = contract(wq_buf[k], x_ref[...], ((0,), (1,))).astype(BF16)


def stretch(tok, picked, w_ada, b_ada, w_qkv):
    count, width = tok.shape
    steps = 3
    cols = 2 * width // steps

    def ada(i):
        return jnp.minimum(i, steps - 1)

    return pl.pallas_call(
        functools.partial(stretch_kernel, steps),
        grid=(steps + 2,),
        in_specs=[
            pl.BlockSpec((count, width), lambda i: (0, 0), pipeline_mode=pl.Buffered(1)),
            pl.BlockSpec((width, cols), lambda i: (0, ada(i))),
            pl.BlockSpec((1, cols), lambda i: (0, ada(i))),
            HBM,
            HBM,
        ],
        out_specs=[
            pl.BlockSpec((width, count), lambda i: (jnp.maximum(i - steps, 0), 0)),
            pl.BlockSpec((count, width), lambda i: (0, 0), pipeline_mode=pl.Buffered(1)),
        ],
        out_shape=[
            jax.ShapeDtypeStruct((2 * width, count), BF16),
            jax.ShapeDtypeStruct((count, width), BF16),
        ],
        scratch_shapes=[
            pltpu.VMEM((count, width), BF16),
            pltpu.VMEM((2, width, width), BF16),
            pltpu.VMEM((count, width), BF16),
            pltpu.VMEM((count, 2 * width), BF16),
            pltpu.SemaphoreType.DMA((3,)),
        ],
        compiler_params=pltpu.CompilerParams(vmem_limit_bytes=58 * MIB),
        cost_estimate=pl.CostEstimate(flops=1, bytes_accessed=1, transcendentals=0),
        name="stretch",
    )(picked, w_ada, b_ada, tok, w_qkv)


def query_kernel(query_scale, place_ref, act_ref, x_ref, ba_ref, wa_ref, wq_ref, *refs):
    q_ref, gate_ref, wa_buf, wq_buf, sems = refs
    count, width = gate_ref.shape
    copies = [
        pltpu.make_async_copy(wq_ref.at[:, :width], wq_buf, sems.at[0]),
        pltpu.make_async_copy(wa_ref.at[:, 2 * width :], wa_buf, sems.at[1]),
    ]
    for copy in copies:
        copy.start()
    mine = pl.ds(pl.multiple_of(place_ref[0] * count, count), count)
    act = jax.nn.silu(act_ref[mine, :].astype(F32)).astype(BF16)
    copies[0].wait()
    q_ref[...] = (contract(wq_buf[...], x_ref[mine, :], ((0,), (1,))) * query_scale).astype(BF16)
    copies[1].wait()
    gate = contract(act, wa_buf[...], ((1,), (0,))) + ba_ref[:, 2 * width :]
    gate_ref[...] = gate.astype(BF16)


def query(place, x, picked, w_ada, b_ada, w_qkv, count):
    width = x.shape[1]
    query_scale = math.log2(math.e) / math.sqrt(width // HEADS)
    return pl.pallas_call(
        functools.partial(query_kernel, query_scale),
        in_specs=[pl.BlockSpec(memory_space=pltpu.SMEM), VMEM, VMEM, VMEM, HBM, HBM],
        out_specs=[VMEM, VMEM],
        out_shape=[
            jax.ShapeDtypeStruct((width, count), BF16),
            jax.ShapeDtypeStruct((count, width), BF16),
        ],
        scratch_shapes=[
            pltpu.VMEM((width, width), BF16),
            pltpu.VMEM((width, width), BF16),
            pltpu.SemaphoreType.DMA((2,)),
        ],
        compiler_params=pltpu.CompilerParams(vmem_limit_bytes=58 * MIB),
        cost_estimate=pl.CostEstimate(flops=1, bytes_accessed=1, transcendentals=0),
        name="query",
    )(place, picked, x, b_ada, w_ada, w_qkv)


def attend_kernel(head_dim, chunk, place_ref, q_ref, *refs):
    kv_refs, (o_ref, s_ref) = refs[:-2], refs[-2:]
    pair, queries = q_ref.shape
    row = lax.broadcasted_iota(jnp.int32, (pair, 1), 0)
    q = q_ref[...]
    zero = jnp.zeros_like(q)
    both = jnp.concatenate(
        [jnp.where(row < head_dim, q, zero), jnp.where(row < head_dim, zero, q)], axis=1
    )
    half = len(kv_refs) // 2
    parts = [
        (k_ref, v_ref, i)
        for k_ref, v_ref in zip(kv_refs[:half], kv_refs[half:])
        for i in range(0, k_ref.shape[1], chunk)
    ]
    top = None
    for n, (k_ref, _, i) in enumerate(parts):
        scores = contract(k_ref[:, i : i + chunk], both, ((0,), (0,)))
        s_ref[n * chunk : (n + 1) * chunk, :] = scores
        peak = jnp.max(scores, axis=0, keepdims=True)
        top = peak if top is None else jnp.maximum(top, peak)
    weighted = denominator = None
    for n, (_, v_ref, i) in enumerate(parts):
        expo = jnp.exp2(s_ref[n * chunk : (n + 1) * chunk, :] - top)
        total = jnp.sum(expo, axis=0, keepdims=True)
        part = contract(v_ref[:, i : i + chunk], expo.astype(BF16), ((1,), (0,)))
        weighted = part if weighted is None else weighted + part
        denominator = total if denominator is None else denominator + total
    result = weighted / denominator
    o_ref[...] = jnp.where(row < head_dim, result[:, :queries], result[:, queries:]).astype(BF16)


def attend(place, which, qt, kvs):
    width, queries = qt.shape[0], qt.shape[1] // 2
    keys = kvs[0].shape[1]
    head_dim = width // HEADS
    pair, pairs = 2 * head_dim, HEADS // 2
    chunk = math.gcd(keys, 512)
    k_spec = pl.BlockSpec((pair, keys), lambda p, place: (p, 0))
    v_spec = pl.BlockSpec((pair, keys), lambda p, place: (p + pairs, 0))
    total = len(kvs) * keys
    return pl.pallas_call(
        functools.partial(attend_kernel, head_dim, chunk),
        grid_spec=pltpu.PrefetchScalarGridSpec(
            num_scalar_prefetch=1,
            grid=(pairs,),
            in_specs=[pl.BlockSpec((pair, queries), lambda p, place: (p, place[which]))]
            + [k_spec] * len(kvs)
            + [v_spec] * len(kvs),
            out_specs=pl.BlockSpec((pair, queries), lambda p, place: (p, 0)),
            scratch_shapes=[pltpu.VMEM((total, 2 * queries), F32)],
        ),
        out_shape=jax.ShapeDtypeStruct((width, queries), BF16),
        compiler_params=pltpu.CompilerParams(vmem_limit_bytes=16 * MIB),
        cost_estimate=pl.CostEstimate(
            flops=16 * total * queries * width,
            bytes_accessed=4 * total * width,
            transcendentals=HEADS * total * queries,
        ),
        name="attend",
    )(place, qt, *kvs, *kvs)


def finish_kernel(place_ref, att_ref, tok_ref, gate_ref, w_ref, o_ref):
    projected = contract(att_ref[...], w_ref[...], ((0,), (0,)))
    o_ref[...] = (tok_ref[...].astype(F32) + gate_ref[...].astype(F32) * projected).astype(BF16)


def finish(place, which, attended, tok, gate, w_out):
    width, queries = attended.shape
    at = pl.BlockSpec((queries, width), lambda i, place: (place[which], 0))
    tok_at = pl.BlockSpec((queries, width), lambda i, place: (2 * place[0] + place[which], 0))
    return pl.pallas_call(
        finish_kernel,
        grid_spec=pltpu.PrefetchScalarGridSpec(
            num_scalar_prefetch=1,
            grid=(1,),
            in_specs=[
                pl.BlockSpec((width, queries), lambda i, place: (0, 0)),
                tok_at,
                at,
                pl.BlockSpec((width, width), lambda i, place: (0, 0)),
            ],
            out_specs=pl.BlockSpec((queries, width), lambda i, place: (0, 0)),
        ),
        out_shape=jax.ShapeDtypeStruct((queries, width), BF16),
        compiler_params=pltpu.CompilerParams(vmem_limit_bytes=12 * MIB),
        name="finish",
    )(place, attended, tok, gate, w_out)


def swap(x, axis, bits):
    return lax.ppermute(x, axis, [(i, i ^ bits) for i in range(lax.axis_size(axis))])


def after(x, *others):
    return lax.optimization_barrier((x, others))[0]


def to_chips(own):
    return {o: swap(own, "region", o) if o else own for o in range(0, lax.axis_size("region"), 2)}


def to_cores(blocks):
    both = blocks | {o ^ 1: swap(b, "region", 1) for o, b in blocks.items()}
    return [both[o] for o in range(len(both))]


def per_device(
    tokens, element_ids, element_slot, live_count, cond_table, w_ada, b_ada, w_qkv, w_out
):
    device_tokens = tokens[0]
    tok_rows, width = device_tokens.shape
    elem_rows = cond_table.shape[0]
    size, n = lax.axis_size("region"), lax.axis_size("ctx")
    h = n // 2
    block = tok_rows // 2
    r, c = lax.axis_index("region"), lax.axis_index("ctx")
    core, upper = r % 2, (c >= h).astype(jnp.int32)
    m = jnp.where(upper == 1, n - 1 - c, c)

    tables = [swap(cond_table, "ctx", d) for d in range(1, n)]
    near = to_chips(after(cond_table, tables[0]))
    mine = lax.dynamic_slice_in_dim(device_tokens, core * block, block)
    other = lax.dynamic_slice_in_dim(device_tokens, (1 - core) * block, block)
    got = swap(other, "region", 1)
    position = jnp.arange(tok_rows, dtype=jnp.int32)
    ids = jnp.where(position < live_count[0, 0], element_ids[0], -1)
    ids = after(ids, tables[0])
    ids = lax.all_to_all(
        jnp.broadcast_to(ids, (n, tok_rows)), "ctx", split_axis=0, concat_axis=0, tiled=True
    )
    tables, near, mine, got = lax.optimization_barrier((tables, near, mine, got))

    far = to_chips(jnp.concatenate(tables, axis=0))
    even, odd = jnp.where(core == 0, mine, got), jnp.where(core == 0, got, mine)
    work, pass_on = jnp.where(upper == 0, even, odd), jnp.where(upper == 0, odd, even)
    same = (jnp.arange(n) >= h).astype(jnp.int32) == upper
    sent = jnp.where(same[:, None, None], work[None], pass_on[None])
    tok = lax.all_to_all(sent, "ctx", split_axis=0, concat_axis=0, tiled=True)
    tok = tok.reshape(n * block, width)

    ids = jnp.where(core == upper, ids, swap(ids, "region", 1))
    ids = lax.dynamic_slice_in_dim(ids, core * block, block, axis=1).reshape(n * block, 1)
    slots = element_slot[jnp.maximum(ids, 0)]
    owner = slots // elem_rows
    relative = ((((owner // n) ^ r) * n) + ((owner % n) ^ c)) * elem_rows + slots % elem_rows
    relative = jnp.where(ids < 0, -1, relative)

    def pick(picked, chips, d):
        order = list(chips) + [o ^ 1 for o in chips]
        pieces = list(chips.values()) + [swap(b, "region", 1) for b in chips.values()]
        bases = [(o * n + d) * elem_rows for o in order]
        return pick_rows(relative, picked, pieces, bases, 2 * block)

    picked = pick([], near, 0)
    far, picked = lax.optimization_barrier((far, picked))
    first = {o: far[o] for o in far if o < size // 2}
    second = {o: far[o] for o in far if o >= size // 2}
    picked = pick([picked], first, 1)
    picked = pick([picked], second, 1)
    tok = after(tok, picked)

    base = jnp.where(upper == 1, n - 2 - 2 * m, 2 * m)
    place = jnp.stack([base // 2, core ^ upper, 1 - core ^ upper]).astype(jnp.int32)
    bias = b_ada.reshape(1, -1)
    kv, x = stretch(tok, picked, w_ada, bias, w_qkv)
    kvs = [kv, swap(kv, "region", 1)]
    qt, gate = query(place, x, picked, w_ada, bias, w_qkv, 2 * block)

    home = []
    for which in (1, 2):
        attended = attend(place, which, qt, kvs)
        if home:
            attended = after(attended, home[0])
        result = finish(place, which, attended, tok, gate, w_out)
        pairs = []
        for region in range(size):
            for k in range(h):
                to = 2 * k + (region % 2 if which == 1 else 1 - region % 2)
                pairs.append((region * n + k, (region & ~1) * n + to))
                pairs.append((region * n + n - 1 - k, (region | 1) * n + n - 1 - to))
        home.append(lax.ppermute(result, ("region", "ctx"), pairs))
    number = jnp.where(core == 1, n - 1 - c, c) % 2
    low, high = jnp.where(number == 0, home[0], home[1]), jnp.where(number == 0, home[1], home[0])
    return jnp.concatenate([low, high], axis=0)[None]


def solution(mesh):
    placed = (
        P("region", "ctx", None),
        P("region", "ctx"),
        P(),
        P("region", "ctx"),
        P(("region", "ctx"), None),
        P(),
        P(),
        P(),
        P(),
    )
    return jax.shard_map(
        per_device, mesh=mesh, in_specs=placed, out_specs=P("region", "ctx", None), check_vma=False
    )
```

```python
import functools
import math

import jax
import jax.numpy as jnp
from jax import lax
from jax.experimental import pallas as pl
from jax.experimental.pallas import tpu as pltpu
from jax.sharding import PartitionSpec as P

HEADS = 16
F32 = jnp.float32
BF16 = jnp.bfloat16
MIB = 2**20


def contract(a, b, dims):
    return lax.dot_general(a, b, (dims, ((), ())), preferred_element_type=F32)


VMEM = pl.BlockSpec(memory_space=pltpu.VMEM)
HBM = pl.BlockSpec(memory_space=pltpu.HBM)


def pick_kernel(bases, block, idx_ref, *refs):
    pieces, (out_ref, rows_ref) = refs[:-2], refs[-2:]
    acc_ref = None
    if len(pieces) > len(bases):
        acc_ref, pieces = pieces[0], pieces[1:]
    rows = pieces[0].shape[0]
    for n, piece in enumerate(pieces):
        rows_ref[n * rows : (n + 1) * rows, :] = piece[...]
    lane = lax.broadcasted_iota(jnp.int32, (1, rows), 1)
    for lo in range(0, out_ref.shape[0], block):
        span = slice(lo, lo + block)
        idx = idx_ref[span, :]
        hot = jnp.concatenate(
            [jnp.where(idx == lane + base, 1.0, 0.0).astype(BF16) for base in bases], axis=1
        )
        picked = contract(hot, rows_ref[...], ((1,), (0,)))
        if acc_ref is not None:
            picked = picked + acc_ref[span, :].astype(F32)
        out_ref[span, :] = picked.astype(BF16)


def pick_rows(idx, acc, pieces, bases, block):
    rows, width = pieces[0].shape
    return pl.pallas_call(
        functools.partial(pick_kernel, bases, block),
        in_specs=[VMEM] * (1 + len(acc) + len(pieces)),
        out_specs=VMEM,
        out_shape=jax.ShapeDtypeStruct((idx.shape[0], width), BF16),
        scratch_shapes=[pltpu.VMEM((len(pieces) * rows, width), BF16)],
        input_output_aliases={1: 0} if acc else {},
        compiler_params=pltpu.CompilerParams(vmem_limit_bytes=16 * MIB),
        cost_estimate=pl.CostEstimate(flops=1, bytes_accessed=1, transcendentals=0),
        name="pick",
    )(idx, *acc, *pieces)


def stretch_kernel(steps, act_ref, wa_ref, ba_ref, tok_ref, wq_ref, kv_ref, x_ref, *scratch):
    tok_buf, wq_buf, silu_ref, mods_ref, sems = scratch
    count, width = x_ref.shape
    cols = wa_ref.shape[1]
    i = pl.program_id(0)
    tok_copy = pltpu.make_async_copy(tok_ref, tok_buf, sems.at[0])
    wq_copies = [
        pltpu.make_async_copy(
            wq_ref.at[:, k * width : (k + 1) * width], wq_buf.at[k - 1], sems.at[k]
        )
        for k in (1, 2)
    ]
    blocks = [slice(lo, lo + 256) for lo in range(0, count, 256)]

    @pl.when(i == 0)
    def _():
        tok_copy.start()
        for copy in wq_copies:
            copy.start()
        for span in blocks:
            silu_ref[span, :] = jax.nn.silu(act_ref[span, :].astype(F32)).astype(BF16)

    for k in range(steps):

        @pl.when(i == k)
        def _():
            mods = contract(silu_ref[...], wa_ref[...], ((1,), (0,))) + ba_ref[...]
            mods_ref[:, k * cols : (k + 1) * cols] = mods.astype(BF16)

    @pl.when(i == steps - 1)
    def _():
        tok_copy.wait()
        for span in blocks:
            values = tok_buf[span, :].astype(F32)
            moved = values - jnp.mean(values, axis=1, keepdims=True)
            spread = jnp.mean(moved * moved, axis=1, keepdims=True)
            normed = moved * lax.rsqrt(spread + 1e-06)
            shift, scale = mods_ref[span, :width], mods_ref[span, width:]
            x_ref[span, :] = (normed * (1.0 + scale.astype(F32)) + shift.astype(F32)).astype(BF16)

    for k, copy in enumerate(wq_copies):

        @pl.when(i == steps + k)
        def _():
            copy.wait()
            kv_ref[...] = contract(wq_buf[k], x_ref[...], ((0,), (1,))).astype(BF16)


def stretch(tok, picked, w_ada, b_ada, w_qkv):
    count, width = tok.shape
    steps = 3
    cols = 2 * width // steps

    def ada(i):
        return jnp.minimum(i, steps - 1)

    return pl.pallas_call(
        functools.partial(stretch_kernel, steps),
        grid=(steps + 2,),
        in_specs=[
            pl.BlockSpec((count, width), lambda i: (0, 0), pipeline_mode=pl.Buffered(1)),
            pl.BlockSpec((width, cols), lambda i: (0, ada(i))),
            pl.BlockSpec((1, cols), lambda i: (0, ada(i))),
            HBM,
            HBM,
        ],
        out_specs=[
            pl.BlockSpec((width, count), lambda i: (jnp.maximum(i - steps, 0), 0)),
            pl.BlockSpec((count, width), lambda i: (0, 0), pipeline_mode=pl.Buffered(1)),
        ],
        out_shape=[
            jax.ShapeDtypeStruct((2 * width, count), BF16),
            jax.ShapeDtypeStruct((count, width), BF16),
        ],
        scratch_shapes=[
            pltpu.VMEM((count, width), BF16),
            pltpu.VMEM((2, width, width), BF16),
            pltpu.VMEM((count, width), BF16),
            pltpu.VMEM((count, 2 * width), BF16),
            pltpu.SemaphoreType.DMA((3,)),
        ],
        compiler_params=pltpu.CompilerParams(vmem_limit_bytes=58 * MIB),
        cost_estimate=pl.CostEstimate(flops=1, bytes_accessed=1, transcendentals=0),
        name="stretch",
    )(picked, w_ada, b_ada, tok, w_qkv)


def query_kernel(query_scale, place_ref, act_ref, x_ref, ba_ref, wa_ref, wq_ref, *refs):
    q_ref, gate_ref, wa_buf, wq_buf, sems = refs
    count, width = gate_ref.shape
    half = count // 2
    copies = [
        pltpu.make_async_copy(wq_ref.at[:, :width], wq_buf, sems.at[0]),
        pltpu.make_async_copy(wa_ref.at[:, 2 * width :], wa_buf, sems.at[1]),
    ]
    for copy in copies:
        copy.start()
    rows = [pl.ds(pl.multiple_of(place_ref[k] * half, half), half) for k in range(2)]
    x = jnp.concatenate([x_ref[span, :] for span in rows], axis=0)
    act = jnp.concatenate([act_ref[span, :] for span in rows], axis=0)
    act = jax.nn.silu(act.astype(F32)).astype(BF16)
    copies[0].wait()
    q_ref[...] = (contract(wq_buf[...], x, ((0,), (1,))) * query_scale).astype(BF16)
    copies[1].wait()
    gate = contract(act, wa_buf[...], ((1,), (0,))) + ba_ref[:, 2 * width :]
    gate_ref[...] = gate.astype(BF16)


def query(place, x, picked, w_ada, b_ada, w_qkv, count):
    width = x.shape[1]
    query_scale = math.log2(math.e) / math.sqrt(width // HEADS)
    return pl.pallas_call(
        functools.partial(query_kernel, query_scale),
        in_specs=[pl.BlockSpec(memory_space=pltpu.SMEM), VMEM, VMEM, VMEM, HBM, HBM],
        out_specs=[VMEM, VMEM],
        out_shape=[
            jax.ShapeDtypeStruct((width, count), BF16),
            jax.ShapeDtypeStruct((count, width), BF16),
        ],
        scratch_shapes=[
            pltpu.VMEM((width, width), BF16),
            pltpu.VMEM((width, width), BF16),
            pltpu.SemaphoreType.DMA((2,)),
        ],
        compiler_params=pltpu.CompilerParams(vmem_limit_bytes=58 * MIB),
        cost_estimate=pl.CostEstimate(flops=1, bytes_accessed=1, transcendentals=0),
        name="query",
    )(place, picked, x, b_ada, w_ada, w_qkv)


def attend_kernel(head_dim, chunk, q_ref, *refs):
    kv_refs, (o_ref, s_ref) = refs[:-2], refs[-2:]
    pair, queries = q_ref.shape
    row = lax.broadcasted_iota(jnp.int32, (pair, 1), 0)
    q = q_ref[...]
    zero = jnp.zeros_like(q)
    both = jnp.concatenate(
        [jnp.where(row < head_dim, q, zero), jnp.where(row < head_dim, zero, q)], axis=1
    )
    half = len(kv_refs) // 2
    parts = [
        (k_ref, v_ref, i)
        for k_ref, v_ref in zip(kv_refs[:half], kv_refs[half:])
        for i in range(0, k_ref.shape[1], chunk)
    ]
    top = None
    for n, (k_ref, _, i) in enumerate(parts):
        scores = contract(k_ref[:, i : i + chunk], both, ((0,), (0,)))
        s_ref[n * chunk : (n + 1) * chunk, :] = scores
        peak = jnp.max(scores, axis=0, keepdims=True)
        top = peak if top is None else jnp.maximum(top, peak)
    weighted = denominator = None
    for n, (_, v_ref, i) in enumerate(parts):
        expo = jnp.exp2(s_ref[n * chunk : (n + 1) * chunk, :] - top)
        total = jnp.sum(expo, axis=0, keepdims=True)
        part = contract(v_ref[:, i : i + chunk], expo.astype(BF16), ((1,), (0,)))
        weighted = part if weighted is None else weighted + part
        denominator = total if denominator is None else denominator + total
    result = weighted / denominator
    o_ref[...] = jnp.where(row < head_dim, result[:, :queries], result[:, queries:]).astype(BF16)


def attend(which, qt, kvs):
    width, queries = qt.shape[0], qt.shape[1] // 2
    keys = kvs[0].shape[1]
    head_dim = width // HEADS
    pair, pairs = 2 * head_dim, HEADS // 2
    chunk = math.gcd(keys, 512)
    k_spec = pl.BlockSpec((pair, keys), lambda p: (p, 0))
    v_spec = pl.BlockSpec((pair, keys), lambda p: (p + pairs, 0))
    total = len(kvs) * keys
    return pl.pallas_call(
        functools.partial(attend_kernel, head_dim, chunk),
        grid=(pairs,),
        in_specs=[pl.BlockSpec((pair, queries), lambda p: (p, which))]
        + [k_spec] * len(kvs)
        + [v_spec] * len(kvs),
        out_specs=pl.BlockSpec((pair, queries), lambda p: (p, 0)),
        out_shape=jax.ShapeDtypeStruct((width, queries), BF16),
        scratch_shapes=[pltpu.VMEM((total, 2 * queries), F32)],
        compiler_params=pltpu.CompilerParams(vmem_limit_bytes=16 * MIB),
        cost_estimate=pl.CostEstimate(
            flops=16 * total * queries * width,
            bytes_accessed=4 * total * width,
            transcendentals=HEADS * total * queries,
        ),
        name="attend",
    )(qt, *kvs, *kvs)


def finish_kernel(place_ref, att_ref, tok_ref, gate_ref, w_ref, o_ref):
    projected = contract(att_ref[...], w_ref[...], ((0,), (0,)))
    o_ref[...] = (tok_ref[...].astype(F32) + gate_ref[...].astype(F32) * projected).astype(BF16)


def finish(place, which, attended, tok, gate, w_out):
    width, queries = attended.shape
    at = pl.BlockSpec((queries, width), lambda i, place: (which, 0))
    tok_at = pl.BlockSpec((queries, width), lambda i, place: (place[which], 0))
    return pl.pallas_call(
        finish_kernel,
        grid_spec=pltpu.PrefetchScalarGridSpec(
            num_scalar_prefetch=1,
            grid=(1,),
            in_specs=[
                pl.BlockSpec((width, queries), lambda i, place: (0, 0)),
                tok_at,
                at,
                pl.BlockSpec((width, width), lambda i, place: (0, 0)),
            ],
            out_specs=pl.BlockSpec((queries, width), lambda i, place: (0, 0)),
        ),
        out_shape=jax.ShapeDtypeStruct((queries, width), BF16),
        compiler_params=pltpu.CompilerParams(vmem_limit_bytes=12 * MIB),
        name="finish",
    )(place, attended, tok, gate, w_out)


def swap(x, axis, bits):
    return lax.ppermute(x, axis, [(i, i ^ bits) for i in range(lax.axis_size(axis))])


def after(x, *others):
    return lax.optimization_barrier((x, others))[0]


def to_chips(own):
    return {o: swap(own, "region", o) if o else own for o in range(0, lax.axis_size("region"), 2)}


def to_cores(blocks):
    both = blocks | {o ^ 1: swap(b, "region", 1) for o, b in blocks.items()}
    return [both[o] for o in range(len(both))]


def per_device(
    tokens, element_ids, element_slot, live_count, cond_table, w_ada, b_ada, w_qkv, w_out
):
    device_tokens = tokens[0]
    tok_rows, width = device_tokens.shape
    elem_rows = cond_table.shape[0]
    size, n = lax.axis_size("region"), lax.axis_size("ctx")
    h = n // 2
    block = tok_rows // 2
    r, c = lax.axis_index("region"), lax.axis_index("ctx")
    core, upper = r % 2, (c >= h).astype(jnp.int32)

    tables = [swap(cond_table, "ctx", d) for d in range(1, n)]
    mine = lax.dynamic_slice_in_dim(device_tokens, core * block, block)
    other = lax.dynamic_slice_in_dim(device_tokens, (1 - core) * block, block)
    got = swap(other, "region", 1)
    own, all_ids = after((cond_table, element_ids[0]), got)
    near = to_chips(own)
    position = jnp.arange(tok_rows, dtype=jnp.int32)
    ids = jnp.where(position < live_count[0, 0], all_ids, -1)
    ids = lax.all_to_all(
        jnp.broadcast_to(ids, (n, tok_rows)), "ctx", split_axis=0, concat_axis=0, tiled=True
    )
    even, odd = jnp.where(core == 0, mine, got), jnp.where(core == 0, got, mine)
    work, pass_on = jnp.where(upper == 0, even, odd), jnp.where(upper == 0, odd, even)
    same = (jnp.arange(n) >= h).astype(jnp.int32) == upper
    sent = jnp.where(same[:, None, None], work[None], pass_on[None])
    tables, near, sent, ids = lax.optimization_barrier((tables, near, sent, ids))

    far = to_chips(jnp.concatenate(tables, axis=0))
    tok = lax.all_to_all(sent, "ctx", split_axis=0, concat_axis=0, tiled=True)
    tok = tok.reshape(n * block, width)

    ids = jnp.where(core == upper, ids, swap(ids, "region", 1))
    ids = lax.dynamic_slice_in_dim(ids, core * block, block, axis=1).reshape(n * block, 1)
    slots = element_slot[jnp.maximum(ids, 0)]
    owner = slots // elem_rows
    relative = ((((owner // n) ^ r) * n) + ((owner % n) ^ c)) * elem_rows + slots % elem_rows
    relative = jnp.where(ids < 0, -1, relative)

    def pick(picked, chips, d):
        order = list(chips) + [o ^ 1 for o in chips]
        pieces = list(chips.values()) + [swap(b, "region", 1) for b in chips.values()]
        bases = [(o * n + d) * elem_rows for o in order]
        return pick_rows(relative, picked, pieces, bases, 2 * block)

    picked = pick([], near, 0)
    far, picked = lax.optimization_barrier((far, picked))
    first = {o: far[o] for o in far if o < size // 2}
    second = {o: far[o] for o in far if o >= size // 2}
    picked = pick([picked], first, 1)
    picked = pick([picked], second, 1)
    tok = after(tok, picked)

    place = jnp.stack([n - 1 - c, c]).astype(jnp.int32)
    bias = b_ada.reshape(1, -1)
    kv, x = stretch(tok, picked, w_ada, bias, w_qkv)
    kvs = [kv, swap(kv, "region", 1)]
    qt, gate = query(place, x, picked, w_ada, bias, w_qkv, 2 * block)

    there = finish(place, 0, attend(0, qt, kvs), tok, gate, w_out)
    low, high = (
        lax.ppermute(
            there,
            ("region", "ctx"),
            [
                ((pair + k) * n + chip, (pair + chip // h) * n + n - 1 - chip)
                for pair in range(0, size, 2)
                for chip in range(n)
            ],
        )
        for k in range(2)
    )
    attended = attend(1, qt, kvs)
    here = finish(place, 1, attended, tok, gate, w_out)
    here, low, high = lax.optimization_barrier((here, low, high))
    other = swap(here, "region", 1)
    own_low, own_high = jnp.where(core == 0, here, other), jnp.where(core == 0, other, here)
    low, high = jnp.where(core == upper, own_low, low), jnp.where(core == upper, own_high, high)
    return jnp.concatenate([low, high], axis=0)[None]


def solution(mesh):
    placed = (
        P("region", "ctx", None),
        P("region", "ctx"),
        P(),
        P("region", "ctx"),
        P(("region", "ctx"), None),
        P(),
        P(),
        P(),
        P(),
    )
    return jax.shard_map(
        per_device, mesh=mesh, in_specs=placed, out_specs=P("region", "ctx", None), check_vma=False
    )
```

```python
import functools
import math

import jax
import jax.numpy as jnp
from jax import lax
from jax.experimental import pallas as pl
from jax.experimental.pallas import tpu as pltpu
from jax.sharding import PartitionSpec as P

HEADS = 16
F32 = jnp.float32
BF16 = jnp.bfloat16
MIB = 2**20


def contract(a, b, dims):
    return lax.dot_general(a, b, (dims, ((), ())), preferred_element_type=F32)


VMEM = pl.BlockSpec(memory_space=pltpu.VMEM)
HBM = pl.BlockSpec(memory_space=pltpu.HBM)


def pick_kernel(bases, block, idx_ref, *refs):
    pieces, (out_ref, rows_ref) = refs[:-2], refs[-2:]
    acc_ref = None
    if len(pieces) > len(bases):
        acc_ref, pieces = pieces[0], pieces[1:]
    rows = pieces[0].shape[0]
    for n, piece in enumerate(pieces):
        rows_ref[n * rows : (n + 1) * rows, :] = piece[...]
    lane = lax.broadcasted_iota(jnp.int32, (1, rows), 1)
    for lo in range(0, out_ref.shape[0], block):
        span = slice(lo, lo + block)
        idx = idx_ref[span, :]
        hot = jnp.concatenate(
            [jnp.where(idx == lane + base, 1.0, 0.0).astype(BF16) for base in bases], axis=1
        )
        picked = contract(hot, rows_ref[...], ((1,), (0,)))
        if acc_ref is not None:
            picked = picked + acc_ref[span, :].astype(F32)
        out_ref[span, :] = picked.astype(BF16)


def pick_rows(idx, acc, pieces, bases, block):
    rows, width = pieces[0].shape
    return pl.pallas_call(
        functools.partial(pick_kernel, bases, block),
        in_specs=[VMEM] * (1 + len(acc) + len(pieces)),
        out_specs=VMEM,
        out_shape=jax.ShapeDtypeStruct((idx.shape[0], width), BF16),
        scratch_shapes=[pltpu.VMEM((len(pieces) * rows, width), BF16)],
        input_output_aliases={1: 0} if acc else {},
        compiler_params=pltpu.CompilerParams(vmem_limit_bytes=16 * MIB),
        cost_estimate=pl.CostEstimate(flops=1, bytes_accessed=1, transcendentals=0),
        name="pick",
    )(idx, *acc, *pieces)


def stretch_kernel(steps, act_ref, wa_ref, ba_ref, tok_ref, wq_ref, kv_ref, x_ref, *scratch):
    tok_buf, wq_buf, silu_ref, mods_ref, sems = scratch
    count, width = x_ref.shape
    cols = wa_ref.shape[1]
    i = pl.program_id(0)
    tok_copy = pltpu.make_async_copy(tok_ref, tok_buf, sems.at[0])
    wq_copies = [
        pltpu.make_async_copy(
            wq_ref.at[:, k * width : (k + 1) * width], wq_buf.at[k - 1], sems.at[k]
        )
        for k in (1, 2)
    ]
    blocks = [slice(lo, lo + 256) for lo in range(0, count, 256)]

    @pl.when(i == 0)
    def _():
        for span in blocks:
            silu_ref[span, :] = jax.nn.silu(act_ref[span, :].astype(F32)).astype(BF16)

    @pl.when(i < steps)
    def _():
        mods = contract(silu_ref[...], wa_ref[...], ((1,), (0,))) + ba_ref[...]
        mods_ref[i] = mods.astype(BF16)

    @pl.when(i == 0)
    def _():
        tok_copy.start()

    @pl.when(i == 1)
    def _():
        for copy in wq_copies:
            copy.start()

    @pl.when(i == steps - 1)
    def _():
        tok_copy.wait()
        for span in blocks:
            values = tok_buf[span, :].astype(F32)
            moved = values - jnp.mean(values, axis=1, keepdims=True)
            spread = jnp.mean(moved * moved, axis=1, keepdims=True)
            normed = moved * lax.rsqrt(spread + 1e-06)
            first = width - cols
            shift = jnp.concatenate([mods_ref[0, span, :], mods_ref[1, span, :first]], axis=1)
            scale = jnp.concatenate([mods_ref[1, span, first:], mods_ref[2, span, :]], axis=1)
            x_ref[span, :] = (normed * (1.0 + scale.astype(F32)) + shift.astype(F32)).astype(BF16)

    for k, copy in enumerate(wq_copies):

        @pl.when(i == steps + k)
        def _():
            copy.wait()

    @pl.when(i >= steps)
    def _():
        kv_ref[...] = contract(wq_buf[i - steps], x_ref[...], ((0,), (1,))).astype(BF16)


def stretch(tok, picked, w_ada, b_ada, w_qkv):
    count, width = tok.shape
    steps = 3
    cols = 2 * width // steps

    def ada(i):
        return jnp.minimum(i, steps - 1)

    return pl.pallas_call(
        functools.partial(stretch_kernel, steps),
        grid=(steps + 2,),
        in_specs=[
            pl.BlockSpec((count, width), lambda i: (0, 0), pipeline_mode=pl.Buffered(1)),
            pl.BlockSpec((width, cols), lambda i: (0, ada(i))),
            pl.BlockSpec((1, cols), lambda i: (0, ada(i))),
            HBM,
            HBM,
        ],
        out_specs=[
            pl.BlockSpec((width, count), lambda i: (jnp.maximum(i - steps, 0), 0)),
            pl.BlockSpec((count, width), lambda i: (0, 0), pipeline_mode=pl.Buffered(1)),
        ],
        out_shape=[
            jax.ShapeDtypeStruct((2 * width, count), BF16),
            jax.ShapeDtypeStruct((count, width), BF16),
        ],
        scratch_shapes=[
            pltpu.VMEM((count, width), BF16),
            pltpu.VMEM((2, width, width), BF16),
            pltpu.VMEM((count, width), BF16),
            pltpu.VMEM((steps, count, cols), BF16),
            pltpu.SemaphoreType.DMA((3,)),
        ],
        compiler_params=pltpu.CompilerParams(vmem_limit_bytes=58 * MIB),
        cost_estimate=pl.CostEstimate(flops=1, bytes_accessed=1, transcendentals=0),
        name="stretch",
    )(picked, w_ada, b_ada, tok, w_qkv)


def query_kernel(query_scale, place_ref, act_ref, x_ref, ba_ref, wa_ref, wq_ref, *refs):
    q_ref, gate_ref, wa_buf, wq_buf, sems = refs
    count, width = gate_ref.shape
    half = count // 2
    copies = [
        pltpu.make_async_copy(wq_ref.at[:, :width], wq_buf, sems.at[0]),
        pltpu.make_async_copy(wa_ref.at[:, 2 * width :], wa_buf, sems.at[1]),
    ]
    for copy in copies:
        copy.start()
    rows = [pl.ds(pl.multiple_of(place_ref[k] * half, half), half) for k in range(2)]
    x = jnp.concatenate([x_ref[span, :] for span in rows], axis=0)
    act = jnp.concatenate([act_ref[span, :] for span in rows], axis=0)
    act = jax.nn.silu(act.astype(F32)).astype(BF16)
    copies[0].wait()
    q_ref[...] = (contract(wq_buf[...], x, ((0,), (1,))) * query_scale).astype(BF16)
    copies[1].wait()
    gate = contract(act, wa_buf[...], ((1,), (0,))) + ba_ref[:, 2 * width :]
    gate_ref[...] = gate.astype(BF16)


def query(place, x, picked, w_ada, b_ada, w_qkv, count):
    width = x.shape[1]
    query_scale = math.log2(math.e) / math.sqrt(width // HEADS)
    return pl.pallas_call(
        functools.partial(query_kernel, query_scale),
        in_specs=[pl.BlockSpec(memory_space=pltpu.SMEM), VMEM, VMEM, VMEM, HBM, HBM],
        out_specs=[VMEM, VMEM],
        out_shape=[
            jax.ShapeDtypeStruct((width, count), BF16),
            jax.ShapeDtypeStruct((count, width), BF16),
        ],
        scratch_shapes=[
            pltpu.VMEM((width, width), BF16),
            pltpu.VMEM((width, width), BF16),
            pltpu.SemaphoreType.DMA((2,)),
        ],
        compiler_params=pltpu.CompilerParams(vmem_limit_bytes=58 * MIB),
        cost_estimate=pl.CostEstimate(flops=1, bytes_accessed=1, transcendentals=0),
        name="query",
    )(place, picked, x, b_ada, w_ada, w_qkv)


def attend_kernel(head_dim, chunk, q_ref, *refs):
    kv_refs, (o_ref, s_ref) = refs[:-2], refs[-2:]
    pair, queries = 2 * head_dim, q_ref.shape[1]
    row = lax.broadcasted_iota(jnp.int32, (pair, 1), 0)
    half = len(kv_refs) // 2
    parts = [
        (k_ref, v_ref, i)
        for k_ref, v_ref in zip(kv_refs[:half], kv_refs[half:])
        for i in range(0, k_ref.shape[1], chunk)
    ]
    groups = [slice(lo, lo + pair) for lo in range(0, q_ref.shape[0], pair)]
    both, top = {}, {}

    def score(g, n):
        if n == 0:
            q = q_ref[groups[g], :]
            zero = jnp.zeros_like(q)
            sides = [jnp.where(row < head_dim, q, zero), jnp.where(row < head_dim, zero, q)]
            both[g] = jnp.concatenate(sides, axis=1)
        k_ref, _, i = parts[n]
        scores = contract(k_ref[groups[g], i : i + chunk], both[g], ((0,), (0,)))
        s_ref[g % 2, n * chunk : (n + 1) * chunk, :] = scores
        peak = jnp.max(scores, axis=0, keepdims=True)
        top[g] = jnp.maximum(top[g], peak) if n else peak

    for n in range(len(parts)):
        score(0, n)
    for g, rows in enumerate(groups):
        weighted = denominator = None
        for n, (_, v_ref, i) in enumerate(parts):
            if g + 1 < len(groups):
                score(g + 1, n)
            expo = jnp.exp2(s_ref[g % 2, n * chunk : (n + 1) * chunk, :] - top[g])
            total = jnp.sum(expo, axis=0, keepdims=True)
            part = contract(v_ref[rows, i : i + chunk], expo.astype(BF16), ((1,), (0,)))
            weighted = weighted + part if n else part
            denominator = denominator + total if n else total
        result = weighted / denominator
        o_ref[rows, :] = jnp.where(row < head_dim, result[:, :queries], result[:, queries:]).astype(
            BF16
        )


def attend(which, qt, kvs):
    width, queries = qt.shape[0], qt.shape[1] // 2
    keys = kvs[0].shape[1]
    head_dim = width // HEADS
    steps = HEADS // 4
    rows = width // steps
    chunk = math.gcd(keys, 1024)
    k_spec = pl.BlockSpec((rows, keys), lambda p: (p, 0))
    v_spec = pl.BlockSpec((rows, keys), lambda p: (p + steps, 0))
    total = len(kvs) * keys
    return pl.pallas_call(
        functools.partial(attend_kernel, head_dim, chunk),
        grid=(steps,),
        in_specs=[pl.BlockSpec((rows, queries), lambda p: (p, which))]
        + [k_spec] * len(kvs)
        + [v_spec] * len(kvs),
        out_specs=pl.BlockSpec((rows, queries), lambda p: (p, 0)),
        out_shape=jax.ShapeDtypeStruct((width, queries), BF16),
        scratch_shapes=[pltpu.VMEM((2, total, 2 * queries), F32)],
        compiler_params=pltpu.CompilerParams(vmem_limit_bytes=8 * MIB + 32 * total * queries),
        cost_estimate=pl.CostEstimate(
            flops=16 * total * queries * width,
            bytes_accessed=4 * total * width,
            transcendentals=HEADS * total * queries,
        ),
        name="attend",
    )(qt, *kvs, *kvs)


def finish_kernel(place_ref, att_ref, tok_ref, gate_ref, w_ref, o_ref):
    projected = contract(att_ref[...], w_ref[...], ((0,), (0,)))
    o_ref[...] = (tok_ref[...].astype(F32) + gate_ref[...].astype(F32) * projected).astype(BF16)


def finish(place, which, attended, tok, gate, w_out):
    width, queries = attended.shape
    at = pl.BlockSpec((queries, width), lambda i, place: (which, 0))
    tok_at = pl.BlockSpec((queries, width), lambda i, place: (place[which], 0))
    return pl.pallas_call(
        finish_kernel,
        grid_spec=pltpu.PrefetchScalarGridSpec(
            num_scalar_prefetch=1,
            grid=(1,),
            in_specs=[
                pl.BlockSpec((width, queries), lambda i, place: (0, 0)),
                tok_at,
                at,
                pl.BlockSpec((width, width), lambda i, place: (0, 0)),
            ],
            out_specs=pl.BlockSpec((queries, width), lambda i, place: (0, 0)),
        ),
        out_shape=jax.ShapeDtypeStruct((queries, width), BF16),
        compiler_params=pltpu.CompilerParams(vmem_limit_bytes=12 * MIB),
        name="finish",
    )(place, attended, tok, gate, w_out)


def swap(x, axis, bits):
    return lax.ppermute(x, axis, [(i, i ^ bits) for i in range(lax.axis_size(axis))])


def after(x, *others):
    return lax.optimization_barrier((x, others))[0]


def to_chips(own):
    return {o: swap(own, "region", o) if o else own for o in range(0, lax.axis_size("region"), 2)}


def to_cores(blocks):
    both = blocks | {o ^ 1: swap(b, "region", 1) for o, b in blocks.items()}
    return [both[o] for o in range(len(both))]


def per_device(
    tokens, element_ids, element_slot, live_count, cond_table, w_ada, b_ada, w_qkv, w_out
):
    device_tokens = tokens[0]
    tok_rows, width = device_tokens.shape
    elem_rows = cond_table.shape[0]
    size, n = lax.axis_size("region"), lax.axis_size("ctx")
    h = n // 2
    block = tok_rows // 2
    r, c = lax.axis_index("region"), lax.axis_index("ctx")
    core, upper = r % 2, (c >= h).astype(jnp.int32)

    tables = [swap(cond_table, "ctx", d) for d in range(1, n)]
    mine = lax.dynamic_slice_in_dim(device_tokens, core * block, block)
    other = lax.dynamic_slice_in_dim(device_tokens, (1 - core) * block, block)
    got = swap(other, "region", 1)
    own, all_ids = after((cond_table, element_ids[0]), got)
    near = to_chips(own)
    position = jnp.arange(tok_rows, dtype=jnp.int32)
    ids = jnp.where(position < live_count[0, 0], all_ids, -1)
    ids = lax.all_to_all(
        jnp.broadcast_to(ids, (n, tok_rows)), "ctx", split_axis=0, concat_axis=0, tiled=True
    )
    even, odd = jnp.where(core == 0, mine, got), jnp.where(core == 0, got, mine)
    work, pass_on = jnp.where(upper == 0, even, odd), jnp.where(upper == 0, odd, even)
    same = (jnp.arange(n) >= h).astype(jnp.int32) == upper
    sent = jnp.where(same[:, None, None], work[None], pass_on[None])
    tables, near, sent, ids = lax.optimization_barrier((tables, near, sent, ids))

    far = to_chips(jnp.concatenate(tables, axis=0))
    tok = lax.all_to_all(sent, "ctx", split_axis=0, concat_axis=0, tiled=True)
    tok = tok.reshape(n * block, width)

    ids = jnp.where(core == upper, ids, swap(ids, "region", 1))
    ids = lax.dynamic_slice_in_dim(ids, core * block, block, axis=1).reshape(n * block, 1)
    slots = element_slot[jnp.maximum(ids, 0)]
    owner = slots // elem_rows
    relative = ((((owner // n) ^ r) * n) + ((owner % n) ^ c)) * elem_rows + slots % elem_rows
    relative = jnp.where(ids < 0, -1, relative)

    def pick(picked, blocks, d):
        bases = [(o * n + d) * elem_rows for o in blocks]
        return pick_rows(relative, picked, list(blocks.values()), bases, 2 * block)

    def other_core(chips):
        return {o ^ 1: swap(b, "region", 1) for o, b in chips.items()}

    picked = pick([], near | other_core(near), 0)
    far, picked = lax.optimization_barrier((far, picked))
    picked = pick([picked], far, 1)
    picked = pick([picked], other_core(far), 1)
    tok = after(tok, picked)

    place = jnp.stack([n - 1 - c, c]).astype(jnp.int32)
    bias = b_ada.reshape(1, -1)
    kv, x = stretch(tok, picked, w_ada, bias, w_qkv)
    kvs = [kv, swap(kv, "region", 1)]
    qt, gate = query(place, x, picked, w_ada, bias, w_qkv, 2 * block)

    there = finish(place, 0, attend(0, qt, kvs), tok, gate, w_out)
    back = swap(there, "ctx", n - 1)
    here = finish(place, 1, attend(1, qt, kvs), tok, gate, w_out)
    here, back = lax.optimization_barrier((here, back))
    mine, given = jnp.where(core == upper, here, back), jnp.where(core == upper, back, here)
    other = swap(given, "region", 1)
    low, high = jnp.where(core == 0, mine, other), jnp.where(core == 0, other, mine)
    return jnp.concatenate([low, high], axis=0)[None]


def solution(mesh):
    placed = (
        P("region", "ctx", None),
        P("region", "ctx"),
        P(),
        P("region", "ctx"),
        P(("region", "ctx"), None),
        P(),
        P(),
        P(),
        P(),
    )
    return jax.shard_map(
        per_device, mesh=mesh, in_specs=placed, out_specs=P("region", "ctx", None), check_vma=False
    )
```

```python
import functools
import math

import jax
import jax.numpy as jnp
from jax import lax
from jax.experimental import pallas as pl
from jax.experimental.pallas import tpu as pltpu
from jax.sharding import PartitionSpec as P

HEADS = 16
F32 = jnp.float32
BF16 = jnp.bfloat16
MIB = 2**20


def contract(a, b, dims):
    return lax.dot_general(a, b, (dims, ((), ())), preferred_element_type=F32)


VMEM = pl.BlockSpec(memory_space=pltpu.VMEM)
HBM = pl.BlockSpec(memory_space=pltpu.HBM)


def pick_kernel(bases, block, idx_ref, *refs):
    pieces, (out_ref, rows_ref) = refs[:-2], refs[-2:]
    acc_ref = None
    if len(pieces) > len(bases):
        acc_ref, pieces = pieces[0], pieces[1:]
    rows = pieces[0].shape[0]
    for n, piece in enumerate(pieces):
        rows_ref[n * rows : (n + 1) * rows, :] = piece[...]
    lane = lax.broadcasted_iota(jnp.int32, (1, rows), 1)
    for lo in range(0, out_ref.shape[0], block):
        span = slice(lo, lo + block)
        idx = idx_ref[span, :]
        hot = jnp.concatenate(
            [jnp.where(idx == lane + base, 1.0, 0.0).astype(BF16) for base in bases], axis=1
        )
        picked = contract(hot, rows_ref[...], ((1,), (0,)))
        if acc_ref is not None:
            picked = picked + acc_ref[span, :].astype(F32)
        out_ref[span, :] = picked.astype(BF16)


def pick_rows(idx, acc, pieces, bases, block):
    rows, width = pieces[0].shape
    return pl.pallas_call(
        functools.partial(pick_kernel, bases, block),
        in_specs=[VMEM] * (1 + len(acc) + len(pieces)),
        out_specs=VMEM,
        out_shape=jax.ShapeDtypeStruct((idx.shape[0], width), BF16),
        scratch_shapes=[pltpu.VMEM((len(pieces) * rows, width), BF16)],
        input_output_aliases={1: 0} if acc else {},
        compiler_params=pltpu.CompilerParams(vmem_limit_bytes=16 * MIB),
        cost_estimate=pl.CostEstimate(flops=1, bytes_accessed=1, transcendentals=0),
        name="pick",
    )(idx, *acc, *pieces)


def stretch_kernel(steps, act_ref, wa_ref, ba_ref, tok_ref, wq_ref, kv_ref, x_ref, *scratch):
    tok_buf, wq_buf, silu_ref, mods_ref, sems = scratch
    count, width = x_ref.shape
    cols = wa_ref.shape[1]
    i = pl.program_id(0)
    tok_copy = pltpu.make_async_copy(tok_ref, tok_buf, sems.at[0])
    wq_copies = [
        pltpu.make_async_copy(
            wq_ref.at[:, k * width : (k + 1) * width], wq_buf.at[k - 1], sems.at[k]
        )
        for k in (1, 2)
    ]
    blocks = [slice(lo, lo + 256) for lo in range(0, count, 256)]

    @pl.when(i == 0)
    def _():
        for span in blocks:
            silu_ref[span, :] = jax.nn.silu(act_ref[span, :].astype(F32)).astype(BF16)

    @pl.when(i < steps)
    def _():
        mods = contract(silu_ref[...], wa_ref[...], ((1,), (0,))) + ba_ref[...]
        mods_ref[i] = mods.astype(BF16)

    @pl.when(i == 0)
    def _():
        tok_copy.start()

    @pl.when(i == 1)
    def _():
        for copy in wq_copies:
            copy.start()

    @pl.when(i == steps - 1)
    def _():
        tok_copy.wait()
        for span in blocks:
            values = tok_buf[span, :].astype(F32)
            moved = values - jnp.mean(values, axis=1, keepdims=True)
            spread = jnp.mean(moved * moved, axis=1, keepdims=True)
            normed = moved * lax.rsqrt(spread + 1e-06)
            first = width - cols
            shift = jnp.concatenate([mods_ref[0, span, :], mods_ref[1, span, :first]], axis=1)
            scale = jnp.concatenate([mods_ref[1, span, first:], mods_ref[2, span, :]], axis=1)
            x_ref[span, :] = (normed * (1.0 + scale.astype(F32)) + shift.astype(F32)).astype(BF16)

    for k, copy in enumerate(wq_copies):

        @pl.when(i == steps + k)
        def _():
            copy.wait()

    @pl.when(i >= steps)
    def _():
        kv_ref[...] = contract(wq_buf[i - steps], x_ref[...], ((0,), (1,))).astype(BF16)


def stretch(tok, picked, w_ada, b_ada, w_qkv):
    count, width = tok.shape
    steps = 3
    cols = 2 * width // steps

    def ada(i):
        return jnp.minimum(i, steps - 1)

    return pl.pallas_call(
        functools.partial(stretch_kernel, steps),
        grid=(steps + 2,),
        in_specs=[
            pl.BlockSpec((count, width), lambda i: (0, 0), pipeline_mode=pl.Buffered(1)),
            pl.BlockSpec((width, cols), lambda i: (0, ada(i))),
            pl.BlockSpec((1, cols), lambda i: (0, ada(i))),
            HBM,
            HBM,
        ],
        out_specs=[
            pl.BlockSpec((width, count), lambda i: (jnp.maximum(i - steps, 0), 0)),
            pl.BlockSpec((count, width), lambda i: (0, 0), pipeline_mode=pl.Buffered(1)),
        ],
        out_shape=[
            jax.ShapeDtypeStruct((2 * width, count), BF16),
            jax.ShapeDtypeStruct((count, width), BF16),
        ],
        scratch_shapes=[
            pltpu.VMEM((count, width), BF16),
            pltpu.VMEM((2, width, width), BF16),
            pltpu.VMEM((count, width), BF16),
            pltpu.VMEM((steps, count, cols), BF16),
            pltpu.SemaphoreType.DMA((3,)),
        ],
        compiler_params=pltpu.CompilerParams(vmem_limit_bytes=58 * MIB),
        cost_estimate=pl.CostEstimate(flops=1, bytes_accessed=1, transcendentals=0),
        name="stretch",
    )(picked, w_ada, b_ada, tok, w_qkv)


def query_kernel(query_scale, place_ref, act_ref, x_ref, ba_ref, wa_ref, wq_ref, *refs):
    q_ref, gate_ref, late_ref, wa_buf, wq_buf, sems = refs
    half, width = gate_ref.shape
    copies = [
        pltpu.make_async_copy(wq_ref.at[:, :width], wq_buf, sems.at[0]),
        pltpu.make_async_copy(wa_ref.at[:, 2 * width :], wa_buf, sems.at[1]),
    ]
    for copy in copies:
        copy.start()
    rows = [pl.ds(pl.multiple_of(place_ref[k] * half, half), half) for k in range(2)]
    x = jnp.concatenate([x_ref[span, :] for span in rows], axis=0)
    act = jax.nn.silu(act_ref[rows[0], :].astype(F32)).astype(BF16)
    late_ref[...] = act_ref[rows[1], :]
    copies[0].wait()
    q_ref[...] = (contract(wq_buf[...], x, ((0,), (1,))) * query_scale).astype(BF16)
    copies[1].wait()
    gate = contract(act, wa_buf[...], ((1,), (0,))) + ba_ref[:, 2 * width :]
    gate_ref[...] = gate.astype(BF16)


def query(place, x, picked, w_ada, b_ada, w_qkv, count):
    width = x.shape[1]
    query_scale = math.log2(math.e) / math.sqrt(width // HEADS)
    return pl.pallas_call(
        functools.partial(query_kernel, query_scale),
        in_specs=[pl.BlockSpec(memory_space=pltpu.SMEM), VMEM, VMEM, VMEM, HBM, HBM],
        out_specs=[VMEM, VMEM, VMEM],
        out_shape=[
            jax.ShapeDtypeStruct((width, count), BF16),
            jax.ShapeDtypeStruct((count // 2, width), BF16),
            jax.ShapeDtypeStruct((count // 2, width), BF16),
        ],
        scratch_shapes=[
            pltpu.VMEM((width, width), BF16),
            pltpu.VMEM((width, width), BF16),
            pltpu.SemaphoreType.DMA((2,)),
        ],
        compiler_params=pltpu.CompilerParams(vmem_limit_bytes=58 * MIB),
        cost_estimate=pl.CostEstimate(flops=1, bytes_accessed=1, transcendentals=0),
        name="query",
    )(place, picked, x, b_ada, w_ada, w_qkv)


def gate_kernel(act_ref, ba_ref, wa_ref, gate_ref, wa_buf, sem):
    width = gate_ref.shape[1]
    copy = pltpu.make_async_copy(wa_ref.at[:, 2 * width :], wa_buf, sem.at[0])
    copy.start()
    act = jax.nn.silu(act_ref[...].astype(F32)).astype(BF16)
    copy.wait()
    gate = contract(act, wa_buf[...], ((1,), (0,))) + ba_ref[:, 2 * width :]
    gate_ref[...] = gate.astype(BF16)


def own_gate(rows, w_ada, b_ada):
    block, width = rows.shape
    return pl.pallas_call(
        gate_kernel,
        in_specs=[VMEM, VMEM, HBM],
        out_specs=VMEM,
        out_shape=jax.ShapeDtypeStruct((block, width), BF16),
        scratch_shapes=[pltpu.VMEM((width, width), BF16), pltpu.SemaphoreType.DMA((1,))],
        compiler_params=pltpu.CompilerParams(vmem_limit_bytes=58 * MIB),
        cost_estimate=pl.CostEstimate(flops=1, bytes_accessed=1, transcendentals=0),
        name="own_gate",
    )(rows, b_ada, w_ada)


def attend_kernel(head_dim, chunk, q_ref, *refs):
    kv_refs, (o_ref, s_ref) = refs[:-2], refs[-2:]
    pair, queries = 2 * head_dim, q_ref.shape[1]
    row = lax.broadcasted_iota(jnp.int32, (pair, 1), 0)
    half = len(kv_refs) // 2
    parts = [
        (k_ref, v_ref, i)
        for k_ref, v_ref in zip(kv_refs[:half], kv_refs[half:])
        for i in range(0, k_ref.shape[1], chunk)
    ]
    groups = [slice(lo, lo + pair) for lo in range(0, q_ref.shape[0], pair)]
    both, top = {}, {}

    def score(g, n):
        if n == 0:
            q = q_ref[groups[g], :]
            zero = jnp.zeros_like(q)
            sides = [jnp.where(row < head_dim, q, zero), jnp.where(row < head_dim, zero, q)]
            both[g] = jnp.concatenate(sides, axis=1)
        k_ref, _, i = parts[n]
        scores = contract(k_ref[groups[g], i : i + chunk], both[g], ((0,), (0,)))
        s_ref[g % 2, n * chunk : (n + 1) * chunk, :] = scores
        peak = jnp.max(scores, axis=0, keepdims=True)
        top[g] = jnp.maximum(top[g], peak) if n else peak

    for n in range(len(parts)):
        score(0, n)
    for g, rows in enumerate(groups):
        weighted = denominator = None
        for n, (_, v_ref, i) in enumerate(parts):
            if g + 1 < len(groups):
                score(g + 1, n)
            expo = jnp.exp2(s_ref[g % 2, n * chunk : (n + 1) * chunk, :] - top[g])
            total = jnp.sum(expo, axis=0, keepdims=True)
            part = contract(v_ref[rows, i : i + chunk], expo.astype(BF16), ((1,), (0,)))
            weighted = weighted + part if n else part
            denominator = denominator + total if n else total
        result = weighted / denominator
        o_ref[rows, :] = jnp.where(row < head_dim, result[:, :queries], result[:, queries:]).astype(
            BF16
        )


def attend(which, qt, kvs):
    width, queries = qt.shape[0], qt.shape[1] // 2
    keys = kvs[0].shape[1]
    head_dim = width // HEADS
    steps = HEADS // 4
    rows = width // steps
    chunk = math.gcd(keys, 1024)
    k_spec = pl.BlockSpec((rows, keys), lambda p: (p, 0))
    v_spec = pl.BlockSpec((rows, keys), lambda p: (p + steps, 0))
    total = len(kvs) * keys
    return pl.pallas_call(
        functools.partial(attend_kernel, head_dim, chunk),
        grid=(steps,),
        in_specs=[pl.BlockSpec((rows, queries), lambda p: (p, which))]
        + [k_spec] * len(kvs)
        + [v_spec] * len(kvs),
        out_specs=pl.BlockSpec((rows, queries), lambda p: (p, 0)),
        out_shape=jax.ShapeDtypeStruct((width, queries), BF16),
        scratch_shapes=[pltpu.VMEM((2, total, 2 * queries), F32)],
        compiler_params=pltpu.CompilerParams(vmem_limit_bytes=8 * MIB + 32 * total * queries),
        cost_estimate=pl.CostEstimate(
            flops=16 * total * queries * width,
            bytes_accessed=4 * total * width,
            transcendentals=HEADS * total * queries,
        ),
        name="attend",
    )(qt, *kvs, *kvs)


def finish_kernel(place_ref, att_ref, tok_ref, gate_ref, w_ref, o_ref):
    projected = contract(att_ref[...], w_ref[...], ((0,), (0,)))
    o_ref[...] = (tok_ref[...].astype(F32) + gate_ref[...].astype(F32) * projected).astype(BF16)


def finish(place, which, attended, tok, gate, w_out):
    width, queries = attended.shape
    at = pl.BlockSpec((queries, width), lambda i, place: (0, 0))
    tok_at = pl.BlockSpec((queries, width), lambda i, place: (place[which], 0))
    return pl.pallas_call(
        finish_kernel,
        grid_spec=pltpu.PrefetchScalarGridSpec(
            num_scalar_prefetch=1,
            grid=(1,),
            in_specs=[
                pl.BlockSpec((width, queries), lambda i, place: (0, 0)),
                tok_at,
                at,
                pl.BlockSpec((width, width), lambda i, place: (0, 0)),
            ],
            out_specs=pl.BlockSpec((queries, width), lambda i, place: (0, 0)),
        ),
        out_shape=jax.ShapeDtypeStruct((queries, width), BF16),
        compiler_params=pltpu.CompilerParams(vmem_limit_bytes=12 * MIB),
        name="finish",
    )(place, attended, tok, gate, w_out)


def swap(x, axis, bits):
    return lax.ppermute(x, axis, [(i, i ^ bits) for i in range(lax.axis_size(axis))])


def after(x, *others):
    return lax.optimization_barrier((x, others))[0]


def to_chips(own):
    return {o: swap(own, "region", o) if o else own for o in range(0, lax.axis_size("region"), 2)}


def to_cores(blocks):
    both = blocks | {o ^ 1: swap(b, "region", 1) for o, b in blocks.items()}
    return [both[o] for o in range(len(both))]


def per_device(
    tokens, element_ids, element_slot, live_count, cond_table, w_ada, b_ada, w_qkv, w_out
):
    device_tokens = tokens[0]
    tok_rows, width = device_tokens.shape
    elem_rows = cond_table.shape[0]
    size, n = lax.axis_size("region"), lax.axis_size("ctx")
    h = n // 2
    block = tok_rows // 2
    r, c = lax.axis_index("region"), lax.axis_index("ctx")
    core, upper = r % 2, (c >= h).astype(jnp.int32)

    tables = [swap(cond_table, "ctx", d) for d in range(1, n)]
    mine = lax.dynamic_slice_in_dim(device_tokens, core * block, block)
    other = lax.dynamic_slice_in_dim(device_tokens, (1 - core) * block, block)
    got = swap(other, "region", 1)
    own, all_ids = after((cond_table, element_ids[0]), got)
    near = to_chips(own)
    position = jnp.arange(tok_rows, dtype=jnp.int32)
    ids = jnp.where(position < live_count[0, 0], all_ids, -1)
    ids = lax.all_to_all(
        jnp.broadcast_to(ids, (n, tok_rows)), "ctx", split_axis=0, concat_axis=0, tiled=True
    )
    even, odd = jnp.where(core == 0, mine, got), jnp.where(core == 0, got, mine)
    work, pass_on = jnp.where(upper == 0, even, odd), jnp.where(upper == 0, odd, even)
    same = (jnp.arange(n) >= h).astype(jnp.int32) == upper
    sent = jnp.where(same[:, None, None], work[None], pass_on[None])
    tables, near, sent, ids = lax.optimization_barrier((tables, near, sent, ids))

    far = to_chips(jnp.concatenate(tables, axis=0))
    tok = lax.all_to_all(sent, "ctx", split_axis=0, concat_axis=0, tiled=True)
    tok = tok.reshape(n * block, width)

    ids = jnp.where(core == upper, ids, swap(ids, "region", 1))
    ids = lax.dynamic_slice_in_dim(ids, core * block, block, axis=1).reshape(n * block, 1)
    slots = element_slot[jnp.maximum(ids, 0)]
    owner = slots // elem_rows
    relative = ((((owner // n) ^ r) * n) + ((owner % n) ^ c)) * elem_rows + slots % elem_rows
    relative = jnp.where(ids < 0, -1, relative)

    def pick(picked, blocks, d):
        bases = [(o * n + d) * elem_rows for o in blocks]
        return pick_rows(relative, picked, list(blocks.values()), bases, 2 * block)

    def other_core(chips):
        return {o ^ 1: swap(b, "region", 1) for o, b in chips.items()}

    picked = pick([], near | other_core(near), 0)
    far, picked = lax.optimization_barrier((far, picked))
    picked = pick([picked], far, 1)
    picked = pick([picked], other_core(far), 1)
    tok = after(tok, picked)

    place = jnp.stack([n - 1 - c, c]).astype(jnp.int32)
    bias = b_ada.reshape(1, -1)
    kv, x = stretch(tok, picked, w_ada, bias, w_qkv)
    kvs = [kv, swap(kv, "region", 1)]
    qt, gate, late = query(place, x, picked, w_ada, bias, w_qkv, 2 * block)

    there = finish(place, 0, attend(0, qt, kvs), tok, gate, w_out)
    back = swap(there, "ctx", n - 1)
    attended = attend(1, qt, kvs)
    late = after(late, there, attended)
    here = finish(place, 1, attended, tok, own_gate(late, w_ada, bias), w_out)
    here, back = lax.optimization_barrier((here, back))
    mine, given = jnp.where(core == upper, here, back), jnp.where(core == upper, back, here)
    other = swap(given, "region", 1)
    low, high = jnp.where(core == 0, mine, other), jnp.where(core == 0, other, mine)
    return jnp.concatenate([low, high], axis=0)[None]


def solution(mesh):
    placed = (
        P("region", "ctx", None),
        P("region", "ctx"),
        P(),
        P("region", "ctx"),
        P(("region", "ctx"), None),
        P(),
        P(),
        P(),
        P(),
    )
    return jax.shard_map(
        per_device, mesh=mesh, in_specs=placed, out_specs=P("region", "ctx", None), check_vma=False
    )
```
